256 devices in a mesh: group: 8 (over z), member: 32 (over x, y, core).
Axes of the slice: x: 4, y: 4, z: 8, core: 2. Of those that a mesh axis runs over, the one named last changes fastest.
Arguments:
- object_tiles: float32 [2, 2, 4096, 16384], P(None, None, 'group', 'member'), may hold values from -1 to 1
- probe_modes: float32 [2, 2, 128, 128], replicated, may hold values from -6 to 6
- measured: float32 [8, 32, 8, 128, 128], P('group', 'member'), may hold values from 1 to 3
- slot_offset: int32 [8, 32, 8, 2], P('group', 'member'), may hold values from 0 to 511, as said below
- slot_count: int32 [8, 32], replicated, may hold values from 1 to 8, as said below
Outputs:
- object_grad: float32 [2, 2, 4096, 16384], P(None, None, 'group', 'member')
- probe_grad: float32 [2, 2, 128, 128], replicated
The draws below stay inside these ranges and needn't reach their ends.
Inputs may be any that keep to these rules, and one draw needn't show every extreme that they name: Every draw has a device with 8 positions; only a device's first slot_count slots are positions. `slot_offset`: on the last tile row the row offsets are at most 384, on the last tile column the column offsets likewise, so every patch lies inside the object; elsewhere a patch may reach into the tiles to the right, below, and below right.
All inputs are finite; a program needn't handle non-finite values.
Results may differ from the reference program's by a relative error of at most 0.00011.
Values sent between devices are 32-bit elements; how exact they have to be, the bound alone decides.
A program may use at most 64 MiB of HBM per device.

```python
import math
import jax
import jax.numpy as jnp
from jax import lax

PATCH = 128
MODES = 2
SLICES = 2
TILE = 512
CAP = 8
ROWS = 4096
COLS = 16384
N_GROUP = 8
N_MEMBER = 32


def draw_slot_count(key, part):
    key = jax.random.fold_in(key, 11)
    first_key, second_key = jax.random.split(key)
    counts = jax.random.randint(first_key, (N_GROUP * N_MEMBER,), 1, CAP + 1)
    chosen_device = jax.random.randint(second_key, (), 0, N_GROUP * N_MEMBER)
    counts = counts.at[chosen_device].set(CAP)
    return counts.reshape(N_GROUP, N_MEMBER).astype(jnp.int32)


def draw_slot_offset(key, part):
    key = jax.random.fold_in(key, 23)
    group_ids = jnp.arange(N_GROUP)[:, None, None]
    member_ids = jnp.arange(N_MEMBER)[None, :, None]
    row_high = jnp.where(group_ids < N_GROUP - 1, TILE, TILE - PATCH + 1)
    col_high = jnp.where(member_ids < N_MEMBER - 1, TILE, TILE - PATCH + 1)
    full_shape = (N_GROUP, N_MEMBER, CAP)
    high = jnp.stack([jnp.broadcast_to(row_high, full_shape), jnp.broadcast_to(col_high, full_shape)], -1)
    values = jax.random.randint(key, (N_GROUP, N_MEMBER, CAP, 2), 0, high)
    values = values.at[0, 0, 0, :].set(TILE - 1).at[0, 0, 1, :].set(0)
    return values.astype(jnp.int32)


def levels(key, dims, cuts, smallest, high):
    loudness, own = 1.0, jax.random.fold_in(key, 6)
    for dim, blocks in cuts:
        heights = jnp.exp(jax.random.uniform(jax.random.fold_in(own, dim), (blocks,), jnp.float32, smallest / len(cuts), high / len(cuts)))
        loudness = loudness * jnp.repeat(heights, dims[dim] // blocks).reshape([-1 if axis == dim else 1 for axis in range(len(dims))])
    return loudness


def bell_draw(key, extent, width, limit, dtype=jnp.bfloat16):
    array = jax.random.normal(key, extent, jnp.float32) * width
    return jnp.minimum(jnp.maximum(array, -limit), limit).astype(dtype)


def setup_inputs(seed: int = 0) -> dict:
    splits = jax.random.split(jax.random.key(seed), 6)
    object_tiles = jnp.clip(jax.random.uniform(splits[0], (SLICES, 2, ROWS, COLS), jnp.float32, -1.0, 1.0) * levels(splits[0], (SLICES, 2, ROWS, COLS), ((2, 8), (3, 32)), -0.4, 0.0), -1.0, 1.0)
    probe_modes = bell_draw(splits[1], (MODES, 2, PATCH, PATCH), 1.0, 6.0, jnp.float32)
    measured = jnp.clip(1.0 + 2.0 * jax.random.uniform(splits[2], (N_GROUP, N_MEMBER, CAP, PATCH, PATCH), jnp.float32) ** levels(splits[2], (N_GROUP, N_MEMBER, CAP, PATCH, PATCH), ((0, 8), (1, 32)), -0.2, 0.2), 1.0, 3.0)
    slot_offset = draw_slot_offset(jax.random.fold_in(splits[5], 71), 0)
    slot_count = draw_slot_count(jax.random.fold_in(splits[5], 71), 0)
    return dict(object_tiles=object_tiles, probe_modes=probe_modes, measured=measured, slot_offset=slot_offset, slot_count=slot_count)


fresnel_rate = 0.5

def kernel_parts(size):
    freq = jnp.arange(size)
    signed = jnp.where(freq >= size // 2, freq - size, freq).astype(jnp.float32)
    phase = -math.pi * fresnel_rate * (signed[:, None] ** 2 + signed[None, :] ** 2) / size
    return (jnp.cos(phase), jnp.sin(phase))

def position_loss(patch_cut, probe_modes, amplitude):
    kernel_real, kernel_imag = kernel_parts(PATCH)
    kernel = kernel_real + 1j * kernel_imag
    wave_field = probe_modes[:, 0] + 1j * probe_modes[:, 1]
    for layer_index in range(SLICES):
        wave_field = wave_field * (patch_cut[layer_index, 0] + 1j * patch_cut[layer_index, 1])
        if layer_index < SLICES - 1:
            wave_field = jnp.fft.ifft2(kernel * jnp.fft.fft2(wave_field, norm='ortho'), norm='ortho')
    far_field = jnp.fft.fft2(wave_field, norm='ortho')
    intensity = lax.optimization_barrier(jnp.sum(jnp.real(far_field) ** 2 + jnp.imag(far_field) ** 2, axis=0))
    return jnp.sum((jnp.sqrt(intensity + 1.0) - amplitude) ** 2)

def reference(object_tiles, probe_modes, measured, slot_offset, slot_count):
    per_device = N_MEMBER * CAP
    gradient_fn = jax.grad(position_loss, argnums=(0, 1))

    def visit(item_index, carry):
        grad_object, grad_probe = carry
        group_index = (item_index // per_device).astype(jnp.int32)
        member_index = (item_index // CAP % N_MEMBER).astype(jnp.int32)
        slot_index = (item_index % CAP).astype(jnp.int32)
        valid = (slot_index < slot_count[group_index, member_index]).astype(jnp.float32)
        row_start = (group_index * TILE + slot_offset[group_index, member_index, slot_index, 0]).astype(jnp.int32)
        col_start = (member_index * TILE + slot_offset[group_index, member_index, slot_index, 1]).astype(jnp.int32)
        zero_index = jnp.int32(0)
        starts = (zero_index, zero_index, row_start, col_start)
        patch_cut = lax.dynamic_slice(object_tiles, starts, (SLICES, 2, PATCH, PATCH))
        amplitude = measured[group_index, member_index, slot_index]
        patch_grad, probe_part = gradient_fn(patch_cut, probe_modes, amplitude)
        current = lax.dynamic_slice(grad_object, starts, (SLICES, 2, PATCH, PATCH))
        grad_object = lax.dynamic_update_slice(grad_object, current + valid * patch_grad, starts)
        return (grad_object, grad_probe + valid * probe_part)
    start_carry = (jnp.zeros(object_tiles.shape, jnp.float32), jnp.zeros(probe_modes.shape, jnp.float32))
    grad_object, grad_probe = lax.fori_loop(0, N_GROUP * N_MEMBER * CAP, visit, start_carry)
    total = jnp.sum(slot_count).astype(jnp.float32)
    return (grad_object, grad_probe / jnp.sqrt(total))
```

```python
import math

import jax
import jax.numpy as jnp
import ml_dtypes
import numpy as np
from jax import lax
from jax.experimental import pallas as pl
from jax.experimental.pallas import tpu as pltpu
from jax.sharding import PartitionSpec as P

MESH = pl.DeviceIdType.MESH
F32 = jnp.float32
BF16 = jnp.bfloat16
FRESNEL_RATE = 0.5
PAIR = 2


def make_tables(size):
    freq = np.arange(size)
    fourier = np.exp(-2j * np.pi * (np.outer(freq, freq) % size) / size) / math.sqrt(size)
    signed = np.where(freq >= size // 2, freq - size, freq).astype(np.float64)
    kernel = np.exp(-1j * np.pi * FRESNEL_RATE * signed**2 / size)
    spread = fourier.conj() @ (kernel[:, None] * fourier)
    spread = 0.5 * (spread + spread.T)
    forms = []
    for matrix in (fourier, spread):
        real, imag = matrix.real, matrix.imag
        forms.append(np.block([[real, -imag], [imag, real]]))
        forms.append(np.block([[real, imag], [-imag, real]]))
    exact = np.stack(forms)
    high = exact.astype(ml_dtypes.bfloat16)
    low = (exact - high.astype(np.float64)).astype(ml_dtypes.bfloat16)
    return np.stack([high, low], axis=1)


def split(x):
    high = x.astype(BF16)
    return high, (x - high.astype(F32)).astype(BF16)


def dot(a, b):
    return jnp.dot(a, b, preferred_element_type=F32)


def two_sided(tables, left, right, waves):
    size = waves[0][0].shape[0]
    x = jnp.concatenate(
        [jnp.concatenate([w[0] for w in waves], axis=1), jnp.concatenate([w[1] for w in waves], axis=1)], axis=0
    )
    high, low = split(x)
    t_high, t_low = tables[left, 0], tables[left, 1]
    t = dot(jnp.concatenate([t_high, t_high, t_low], axis=1), jnp.concatenate([high, low, high], axis=0))
    rows = []
    for j in range(len(waves)):
        cols = slice(j * size, (j + 1) * size)
        rows.append(jnp.concatenate([t[:size, cols], t[size:, cols]], axis=1))
    high, low = split(jnp.concatenate(rows, axis=0))
    t_high, t_low = tables[right, 0], tables[right, 1]
    y = dot(jnp.concatenate([high, low, high], axis=1), jnp.concatenate([t_high, t_high, t_low], axis=0))
    return [(y[j * size : (j + 1) * size, :size], y[j * size : (j + 1) * size, size:]) for j in range(len(waves))]


def times(a, b):
    return a[0] * b[0] - a[1] * b[1], a[0] * b[1] + a[1] * b[0]


def conj_times(a, b):
    return a[0] * b[0] + a[1] * b[1], a[0] * b[1] - a[1] * b[0]


def plus(a, b):
    return a[0] + b[0], a[1] + b[1]


def kernel(
    ng,
    nm,
    tile,
    size,
    cap,
    offset_ref,
    count_ref,
    counts_ref,
    object_ref,
    probe_ref,
    measured_ref,
    tables,
    grad_ref,
    probe_grad_ref,
    ext_a,
    ext_b,
    gext,
    land_row,
    land_col,
    land_corner,
    probe_rolled,
    first_cut,
    wave_mid,
    wave_back,
    pieces,
    probe_acc,
    land_pair,
    land_plane,
    land_line,
    shard,
    probe_sum,
    in_send,
    in_recv,
    own_sem,
    out_send,
    out_recv,
    write_sem,
    pair_sem,
    plane_send,
    plane_recv,
    line_send,
    line_recv,
    back_send,
    back_recv,
):
    g, m = lax.axis_index("group"), lax.axis_index("member")
    left, right = (g, lax.rem(m + nm - 1, nm)), (g, lax.rem(m + 1, nm))
    up, down = (lax.rem(g + ng - 1, ng), m), (lax.rem(g + 1, ng), m)
    core, chip = lax.rem(m, 2), m // 2
    chips = nm // 2
    blocks = tile // size
    modes = probe_ref.shape[0] // 2
    ext = (ext_a, ext_b)

    def remote(src, dst, send, recv, device):
        return pltpu.make_async_remote_copy(
            src_ref=src, dst_ref=dst, send_sem=send, recv_sem=recv, device_id=device, device_id_type=MESH
        )

    barrier = pltpu.get_barrier_semaphore()
    low, wide, edge = pl.ds(tile, size), pl.ds(0, tile), pl.ds(0, size)
    rest = pl.ds(size, tile - size)
    own_copies = [
        [
            pltpu.make_async_copy(object_ref.at[s, :, :, pl.ds(j * size, size)], ext[s].at[j, :, wide], own_sem.at[s, j])
            for j in range(blocks)
        ]
        for s in range(2)
    ]
    for copy in own_copies[0] + own_copies[1]:
        copy.start()
    greeted = [left, right]
    greeted += [(g, 2 * lax.rem(chip + d, chips) + core) for d in range(1, chips)]
    greeted += [(lax.rem(g + d, ng), m) for d in range(1, ng)]
    for device in greeted:
        pl.semaphore_signal(barrier, inc=1, device_id=device, device_id_type=MESH)
    pl.semaphore_wait(barrier, len(greeted))

    rims = []
    for s in range(2):
        rims.append(
            [
                remote(object_ref.at[s, :, edge, pl.ds(j * size, size)], ext[s].at[j, :, low], in_send.at[s, j], in_recv.at[s, j], up)
                for j in range(blocks)
            ]
            + [
                remote(object_ref.at[s, :, :, edge], ext[s].at[blocks, :, wide], in_send.at[s, blocks], in_recv.at[s, blocks], left),
                remote(ext[s].at[0, :, low], ext[s].at[blocks, :, low], in_send.at[s, blocks + 1], in_recv.at[s, blocks + 1], left),
            ]
        )
        for copy in rims[s][: blocks + 1]:
            copy.start()

    def place(p):
        row, col = offset_ref[p, 0], offset_ref[p, 1]
        return row, col // size, lax.rem(col, size)

    def roll_probe(p, carry):
        _, _, cs = place(p)
        for plane in range(2 * modes):
            probe_rolled[p, plane] = pltpu.roll(probe_ref[plane], cs, axis=1)
        return carry

    lax.fori_loop(0, cap, roll_probe, 0)

    def from_start(cs):
        return lax.broadcasted_iota(jnp.int32, (size, size), 1) >= cs

    def cut(p, s):
        row, bj, cs = place(p)
        inside = from_start(cs)
        rows = pl.ds(row, size)
        return tuple(jnp.where(inside, ext[s][bj, plane, rows], ext[s][bj + 1, plane, rows]) for plane in range(2))

    def waves_of(ref, p):
        return [(ref[p, 2 * k], ref[p, 2 * k + 1]) for k in range(modes)]

    def store_waves(ref, p, waves):
        for k in range(modes):
            ref[p, 2 * k] = waves[k][0]
            ref[p, 2 * k + 1] = waves[k][1]

    def store_pieces(p, grad):
        _, _, cs = place(p)
        inside = from_start(cs)
        for plane in range(2):
            pieces[p, 0, plane, pl.ds(size, size)] = jnp.where(inside, grad[plane], 0.0)
            pieces[p, 1, plane, pl.ds(size, size)] = jnp.where(inside, 0.0, grad[plane])

    def clear_pieces(p, carry):
        for n in (0, 2):
            pieces[p, :, :, pl.ds(n * size, size)] = jnp.zeros((2, 2, size, size), F32)
        return carry

    lax.fori_loop(0, cap, clear_pieces, 0)

    def assemble(s, i, j):
        total = None
        for p in range(cap):
            row, bj, _ = place(p)
            b = j - bj
            inside = (b >= 0) & (b <= 1)
            start = jnp.where(inside, jnp.clip((i + 1) * size - row, 0, 2 * size), 0)
            part = pieces[p, jnp.where(inside, b, 0), :, pl.ds(start, size)]
            total = part if total is None else total + part
        gext[
            s, :, pl.ds(pl.multiple_of(i * size, size), size), pl.ds(pl.multiple_of(j * size, size), size)
        ] = total

    def assemble_many(s, n, where):
        def one(t, carry):
            assemble(s, *where(t))
            return carry

        lax.fori_loop(0, n, one, 0)

    fourier, fourier_conj, spread, spread_conj = (0, 1), (1, 0), (2, 3), (3, 2)

    def arrive(s):
        rims[s][0].wait_recv()
        rims[s][blocks + 1].start()
        for copy in own_copies[s]:
            copy.wait()
        for copy in rims[s][1:]:
            copy.wait_recv()

    arrive(0)

    def stage_one(t, carry):
        waves = []
        for q in range(PAIR):
            p = t * PAIR + q
            patch = cut(p, 0)
            first_cut[p, 0], first_cut[p, 1] = patch
            waves += [times(w, patch) for w in waves_of(probe_rolled, p)]
        waves = two_sided(tables, *spread, waves)
        for q in range(PAIR):
            store_waves(wave_mid, t * PAIR + q, waves[q * modes : (q + 1) * modes])
        return carry

    lax.fori_loop(0, cap // PAIR, stage_one, 0)

    arrive(1)

    own_count = count_ref[g, m]

    def stage_two(t, carry):
        patches, mids, waves = [], [], []
        for q in range(PAIR):
            p = t * PAIR + q
            patches.append(cut(p, 1))
            mids.append(waves_of(wave_mid, p))
            waves += [times(w, patches[q]) for w in mids[q]]
        far = two_sided(tables, *fourier, waves)
        waves = []
        for q in range(PAIR):
            p = t * PAIR + q
            intensity = None
            for w in far[q * modes : (q + 1) * modes]:
                power = w[0] * w[0] + w[1] * w[1]
                intensity = power if intensity is None else intensity + power
            valid = jnp.where(p < own_count, 2.0, 0.0).astype(F32)
            slope = valid * (1.0 - measured_ref[p] * lax.rsqrt(intensity + 1.0))
            waves += [(w[0] * slope, w[1] * slope) for w in far[q * modes : (q + 1) * modes]]
        back = two_sided(tables, *fourier_conj, waves)
        for q in range(PAIR):
            p = t * PAIR + q
            own = back[q * modes : (q + 1) * modes]
            grad = None
            for mid, w in zip(mids[q], own):
                term = conj_times(mid, w)
                grad = term if grad is None else plus(grad, term)
            store_pieces(p, grad)
            store_waves(wave_back, p, [conj_times(patches[q], w) for w in own])
        return carry

    lax.fori_loop(0, cap // PAIR, stage_two, 0)

    homes = []
    for s in range(2):
        homes.append(
            (
                remote(gext.at[s, :, low, rest], land_row.at[s, :, :, rest], out_send.at[s, 0], out_recv.at[s, 0], down),
                remote(gext.at[s, :, low, low], land_corner.at[s], out_send.at[s, 1], out_recv.at[s, 1], right),
                remote(gext.at[s, :, wide, low], land_col.at[s], out_send.at[s, 2], out_recv.at[s, 2], right),
                remote(gext.at[s, :, low, edge], land_row.at[s, :, :, edge], out_send.at[s, 3], out_recv.at[s, 3], down),
            )
        )

    def send_rims(s):
        assemble_many(s, blocks, lambda t: (blocks, t + 1))
        homes[s][1].start()
        homes[s][0].start()
        assemble_many(s, blocks, lambda t: (t, blocks))
        homes[s][2].start()
        assemble(s, blocks, 0)

    def send_corner(s):
        homes[s][1].wait_recv()
        gext[s, :, low, edge] += land_corner[s]
        homes[s][3].start()

    send_rims(1)
    send_corner(1)
    assemble_many(1, blocks * blocks, lambda t: (t // blocks, lax.rem(t, blocks)))

    probe_acc[...] = jnp.zeros(probe_acc.shape, F32)

    def stage_three(t, carry):
        waves = []
        for q in range(PAIR):
            waves += waves_of(wave_back, t * PAIR + q)
        waves = two_sided(tables, *spread_conj, waves)
        turned_back = [[] for _ in range(PAIR * modes)]
        for q in range(PAIR):
            p = t * PAIR + q
            patch = (first_cut[p, 0], first_cut[p, 1])
            grad = None
            for k, (probe, w) in enumerate(zip(waves_of(probe_rolled, p), waves[q * modes : (q + 1) * modes])):
                term = conj_times(probe, w)
                grad = term if grad is None else plus(grad, term)
                turned = turned_back[q * modes + k]
                for plane, x in enumerate(conj_times(patch, w)):
                    turned.append(x)
            store_pieces(p, grad)
        for k in range(modes):
            for plane in range(2):
                total = None
                for q in range(PAIR):
                    _, _, cs = place(t * PAIR + q)
                    x = pltpu.roll(turned_back[q * modes + k][plane], lax.rem(size - cs, size), axis=1)
                    total = x if total is None else total + x
                probe_acc[pl.ds((2 * k + plane) * size, size), :] += total
        return carry

    lax.fori_loop(0, cap // PAIR, stage_three, 0)
    send_rims(0)

    rows = probe_acc.shape[0]
    half, step = rows // 2, rows // 2 // chips
    partner = (g, m + 1 - 2 * core)
    pair = remote(
        probe_acc.at[pl.ds(pl.multiple_of((1 - core) * half, half), half)], land_pair, pair_sem.at[0], pair_sem.at[1], partner
    )
    pair.start()
    send_corner(0)
    pair.wait_recv()
    mine = pl.ds(pl.multiple_of(core * half, half), half)
    land_pair[...] += probe_acc[mine]
    to_plane, to_line, to_back = [], [], []
    for d in range(1, chips):
        other = lax.rem(chip + d, chips)
        to_plane.append(
            remote(
                land_pair.at[pl.ds(pl.multiple_of(other * step, step), step)],
                land_plane.at[chip],
                plane_send.at[d],
                plane_recv.at[d],
                (g, 2 * other + core),
            )
        )
        to_plane[-1].start()
    land_plane[chip] = land_pair[pl.ds(pl.multiple_of(chip * step, step), step)]
    assemble_many(0, blocks * blocks, lambda t: (t // blocks, lax.rem(t, blocks)))
    for copy in to_plane:
        copy.wait_recv()
    total = land_plane[0]
    for n in range(1, chips):
        total = total + land_plane[n]
    shard[...] = total
    land_line[g] = total
    for d in range(1, ng):
        to_line.append(
            remote(shard, land_line.at[g], line_send.at[d], line_recv.at[d], (lax.rem(g + d, ng), m))
        )
        to_line[-1].start()
    positions = jnp.sum(counts_ref[...].astype(F32), keepdims=True)
    for copy in to_line:
        copy.wait_recv()
    total = land_line[0]
    for n in range(1, ng):
        total = total + land_line[n]
    spot = pl.ds(pl.multiple_of(core * half + chip * step, step), step)
    probe_sum[spot] = total / jnp.sqrt(positions)
    for d in range(1, chips):
        other = lax.rem(chip + d, chips)
        to_back.append(
            remote(probe_sum.at[spot], probe_sum.at[spot], back_send.at[d], back_recv.at[d], (g, 2 * other + core))
        )
        to_back[-1].start()

    writes = []

    def finish(s):
        for n in (0, 2, 3):
            homes[s][n].wait_recv()
        gext[s, :, pl.ds(0, size), wide] += land_row[s]
        gext[s, :, wide, pl.ds(0, size)] += land_col[s]
        writes.append(pltpu.make_async_copy(gext.at[s, :, wide, wide], grad_ref.at[s], write_sem.at[s]))
        writes[-1].start()

    finish(1)
    for copy in to_back:
        copy.wait_recv()
    share = remote(probe_sum.at[mine], probe_sum.at[mine], pair_sem.at[2], pair_sem.at[3], partner)
    share.start()
    finish(0)
    share.wait_recv()
    for plane in range(2 * modes):
        probe_grad_ref[plane] = probe_sum[pl.ds(plane * size, size), :]

    for s in range(2):
        for copy in [*rims[s], *homes[s]]:
            copy.wait_send()
    for copy in to_plane + to_line + to_back + [pair, share]:
        copy.wait_send()
    for copy in writes:
        copy.wait()


def per_device(object_tiles, probe_modes, measured, slot_offset, slot_count):
    ng, nm = lax.axis_size("group"), lax.axis_size("member")
    tile = object_tiles.shape[-1]
    size = probe_modes.shape[-1]
    cap = measured.shape[2]
    planes = 2 * probe_modes.shape[0]
    ext = tile + size
    blocks = tile // size
    chips = nm // 2
    rows = planes * size
    step = rows // 2 // chips
    tables = jnp.asarray(make_tables(size))
    vmem, smem = pl.BlockSpec(memory_space=pltpu.VMEM), pl.BlockSpec(memory_space=pltpu.SMEM)
    hbm = pl.BlockSpec(memory_space=pl.ANY)
    dma = pltpu.SemaphoreType.DMA

    def body(*refs):
        kernel(ng, nm, tile, size, cap, *refs)

    grad, probe_grad = pl.pallas_call(
        body,
        out_shape=(
            jax.ShapeDtypeStruct(object_tiles.shape, F32),
            jax.ShapeDtypeStruct((planes, size, size), F32),
        ),
        in_specs=[smem, smem, vmem, hbm, vmem, vmem, vmem],
        out_specs=(hbm, vmem),
        scratch_shapes=[
            pltpu.VMEM((blocks + 1, 2, ext, size), F32),
            pltpu.VMEM((blocks + 1, 2, ext, size), F32),
            pltpu.VMEM((2, 2, ext, ext), F32),
            pltpu.VMEM((2, 2, size, tile), F32),
            pltpu.VMEM((2, 2, tile, size), F32),
            pltpu.VMEM((2, 2, size, size), F32),
            pltpu.VMEM((cap, planes, size, size), F32),
            pltpu.VMEM((cap, 2, size, size), F32),
            pltpu.VMEM((cap, planes, size, size), F32),
            pltpu.VMEM((cap, planes, size, size), F32),
            pltpu.VMEM((cap, 2, 2, 3 * size, size), F32),
            pltpu.VMEM((rows, size), F32),
            pltpu.VMEM((rows // 2, size), F32),
            pltpu.VMEM((chips, step, size), F32),
            pltpu.VMEM((ng, step, size), F32),
            pltpu.VMEM((step, size), F32),
            pltpu.VMEM((rows, size), F32),
            dma((2, blocks + 2)),
            dma((2, blocks + 2)),
            dma((2, blocks)),
            dma((2, 4)),
            dma((2, 4)),
            dma((2,)),
            dma((4,)),
            dma((chips,)),
            dma((chips,)),
            dma((ng,)),
            dma((ng,)),
            dma((chips,)),
            dma((chips,)),
        ],
        compiler_params=pltpu.CompilerParams(
            collective_id=0, has_side_effects=True, vmem_limit_bytes=48 * 1024 * 1024
        ),
    )(
        slot_offset.reshape(cap, 2),
        slot_count,
        slot_count,
        object_tiles,
        probe_modes.reshape(planes, size, size),
        measured.reshape(cap, size, size),
        tables,
    )
    return grad, probe_grad.reshape(probe_modes.shape)


def solution(mesh):
    placed = (
        P(None, None, "group", "member"),
        P(),
        P("group", "member", None, None, None),
        P("group", "member", None, None),
        P(),
    )
    return jax.shard_map(
        per_device,
        mesh=mesh,
        in_specs=placed,
        out_specs=(P(None, None, "group", "member"), P()),
        check_vma=False,
    )
```

```python
import math

import jax
import jax.numpy as jnp
import ml_dtypes
import numpy as np
from jax import lax
from jax.experimental import pallas as pl
from jax.experimental.pallas import tpu as pltpu
from jax.sharding import PartitionSpec as P

MESH = pl.DeviceIdType.MESH
F32 = jnp.float32
BF16 = jnp.bfloat16
FRESNEL_RATE = 0.5
PAIR = 4


def make_tables(size):
    freq = np.arange(size)
    fourier = np.exp(-2j * np.pi * (np.outer(freq, freq) % size) / size) / math.sqrt(size)
    signed = np.where(freq >= size // 2, freq - size, freq).astype(np.float64)
    kernel = np.exp(-1j * np.pi * FRESNEL_RATE * signed**2 / size)
    spread = fourier.conj() @ (kernel[:, None] * fourier)
    spread = 0.5 * (spread + spread.T)
    forms = []
    for matrix in (fourier, spread):
        real, imag = matrix.real, matrix.imag
        forms.append(np.block([[real, -imag], [imag, real]]))
        forms.append(np.block([[real, imag], [-imag, real]]))
    exact = np.stack(forms)
    high = exact.astype(ml_dtypes.bfloat16)
    low = (exact - high.astype(np.float64)).astype(ml_dtypes.bfloat16)
    return np.stack([high, low], axis=1)


def split(x):
    high = x.astype(BF16)
    return high, (x - high.astype(F32)).astype(BF16)


def dot(a, b):
    return jnp.dot(a, b, preferred_element_type=F32)


def two_sided(tables, left, right, waves):
    size = waves[0][0].shape[0]
    x = jnp.concatenate(
        [jnp.concatenate([w[0] for w in waves], axis=1), jnp.concatenate([w[1] for w in waves], axis=1)], axis=0
    )
    high, low = split(x)
    t_high, t_low = tables[left, 0], tables[left, 1]
    t = dot(jnp.concatenate([t_high, t_high, t_low], axis=1), jnp.concatenate([high, low, high], axis=0))
    rows = []
    for j in range(len(waves)):
        cols = slice(j * size, (j + 1) * size)
        rows.append(jnp.concatenate([t[:size, cols], t[size:, cols]], axis=1))
    high, low = split(jnp.concatenate(rows, axis=0))
    t_high, t_low = tables[right, 0], tables[right, 1]
    y = dot(jnp.concatenate([high, low, high], axis=1), jnp.concatenate([t_high, t_high, t_low], axis=0))
    return [(y[j * size : (j + 1) * size, :size], y[j * size : (j + 1) * size, size:]) for j in range(len(waves))]


def times(a, b):
    return a[0] * b[0] - a[1] * b[1], a[0] * b[1] + a[1] * b[0]


def conj_times(a, b):
    return a[0] * b[0] + a[1] * b[1], a[0] * b[1] - a[1] * b[0]


def plus(a, b):
    return a[0] + b[0], a[1] + b[1]


def kernel(
    ng,
    nm,
    tile,
    size,
    cap,
    offset_hbm,
    counts_hbm,
    object_ref,
    probe_hbm,
    measured_hbm,
    tables_hbm,
    grad_ref,
    probe_grad_ref,
    offset_ref,
    count_ref,
    counts_ref,
    probe_ref,
    measured_ref,
    tables,
    load_sem,
    ext_a,
    ext_b,
    rim_row,
    rim_col,
    land_row,
    land_col,
    land_corner,
    probe_rolled,
    first_cut,
    wave_mid,
    wave_back,
    pieces,
    probe_acc,
    land_pair,
    land_plane,
    part_sum,
    land_z,
    probe_sum,
    in_send,
    in_recv,
    own_sem,
    out_send,
    out_recv,
    pair_sem,
    plane_send,
    plane_recv,
    z_send,
    z_recv,
    back_send,
    back_recv,
):
    g, m = lax.axis_index("group"), lax.axis_index("member")
    left, right = (g, lax.rem(m + nm - 1, nm)), (g, lax.rem(m + 1, nm))
    up, down = (lax.rem(g + ng - 1, ng), m), (lax.rem(g + 1, ng), m)
    core, chip = lax.rem(m, 2), m // 2
    chips = nm // 2
    partner = (g, m + 1 - 2 * core)
    blocks = tile // size
    modes = probe_ref.shape[0] // 2
    ext = (ext_a, ext_b)

    def spot_of(start, length):
        return pl.ds(pl.multiple_of(start, 8), length)

    def remote(src, dst, send, recv, device):
        return pltpu.make_async_remote_copy(
            src_ref=src, dst_ref=dst, send_sem=send, recv_sem=recv, device_id=device, device_id_type=MESH
        )

    barrier = pltpu.get_barrier_semaphore()
    low, wide, edge = pl.ds(tile, size), pl.ds(0, tile), pl.ds(0, size)
    rest = pl.ds(size, tile - size)
    own_copies = [
        [
            pltpu.make_async_copy(object_ref.at[s, :, :, pl.ds(j * size, size)], ext[s].at[j, :, wide], own_sem.at[s, j])
            for j in range(blocks)
        ]
        for s in range(2)
    ]
    greeted = [up, down, left, right]
    greeted += [(g, 2 * lax.rem(chip + d, chips) + core) for d in range(1, chips)]
    greeted += [(lax.rem(g + d, ng), m) for d in range(2, ng - 1)]
    for device in greeted:
        pl.semaphore_signal(barrier, inc=1, device_id=device, device_id_type=MESH)
    loads = [
        pltpu.make_async_copy(src, dst, load_sem.at[n])
        for n, (src, dst) in enumerate(
            (
                (offset_hbm, offset_ref),
                (probe_hbm, probe_ref),
                (tables_hbm, tables),
                (measured_hbm, measured_ref),
                (counts_hbm, count_ref),
                (counts_hbm, counts_ref),
            )
        )
    ]
    for copy in loads + own_copies[0] + own_copies[1]:
        copy.start()
    pl.semaphore_wait(barrier, len(greeted))

    rims = []
    for s in range(2):
        rims.append(
            [
                remote(object_ref.at[s, :, edge, pl.ds(j * size, size)], ext[s].at[j, :, low], in_send.at[s, j], in_recv.at[s, j], up)
                for j in range(blocks)
            ]
            + [
                remote(object_ref.at[s, :, :, edge], ext[s].at[blocks, :, wide], in_send.at[s, blocks], in_recv.at[s, blocks], left),
                remote(ext[s].at[0, :, low], ext[s].at[blocks, :, low], in_send.at[s, blocks + 1], in_recv.at[s, blocks + 1], left),
            ]
        )
        for copy in rims[s][: blocks + 1]:
            copy.start()

    def place(p):
        row, col = offset_ref[0, 0, 0, p], offset_ref[0, 0, 1, p]
        return row, col // size, lax.rem(col, size)

    for copy in loads:
        copy.wait()

    def roll_probe(p, carry):
        _, _, cs = place(p)
        for plane in range(2 * modes):
            probe_rolled[p, plane] = pltpu.roll(probe_ref[plane], cs, axis=1)
        return carry

    lax.fori_loop(0, cap, roll_probe, 0)

    def from_start(cs):
        return lax.broadcasted_iota(jnp.int32, (size, size), 1) >= cs

    def cut(p, s):
        row, bj, cs = place(p)
        inside = from_start(cs)
        rows = pl.ds(row, size)
        return tuple(jnp.where(inside, ext[s][bj, plane, rows], ext[s][bj + 1, plane, rows]) for plane in range(2))

    def waves_of(ref, p):
        return [(ref[p, 2 * k], ref[p, 2 * k + 1]) for k in range(modes)]

    def store_waves(ref, p, waves):
        for k in range(modes):
            ref[p, 2 * k] = waves[k][0]
            ref[p, 2 * k + 1] = waves[k][1]

    def store_pieces(s, p, grad):
        _, _, cs = place(p)
        inside = from_start(cs)
        for plane in range(2):
            pieces[s, p, 0, plane, pl.ds(size, size)] = jnp.where(inside, grad[plane], 0.0)
            pieces[s, p, 1, plane, pl.ds(size, size)] = jnp.where(inside, 0.0, grad[plane])

    def clear_pieces(p, carry):
        for n in (0, 2):
            for s in range(2):
                pieces[s, p, :, :, pl.ds(n * size, size)] = jnp.zeros((2, 2, size, size), F32)
        return carry

    lax.fori_loop(0, cap, clear_pieces, 0)

    def assemble(s, i, j):
        total = None
        for p in range(cap):
            row, bj, _ = place(p)
            b = j - bj
            inside = (b >= 0) & (b <= 1)
            start = jnp.where(inside, jnp.clip((i + 1) * size - row, 0, 2 * size), 0)
            part = pieces[s, p, jnp.where(inside, b, 0), :, pl.ds(start, size)]
            total = part if total is None else total + part
        return total

    def span(t):
        return pl.ds(pl.multiple_of(t * size, size), size)

    def assemble_low(s, j):
        rim_row[s, :, :, span(j)] = assemble(s, blocks, j)

    def assemble_wide(s, i):
        rim_col[s, :, span(i)] = assemble(s, i, blocks)

    def assemble_own(s, t):
        i, j = t // blocks, lax.rem(t, blocks)
        grad_ref[s, :, span(i), span(j)] = assemble(s, i, j)

    def assemble_many(s, n, one):
        def step(t, carry):
            one(s, t)
            return carry

        lax.fori_loop(0, n, step, 0)

    fourier, fourier_conj, spread, spread_conj = (0, 1), (1, 0), (2, 3), (3, 2)

    def arrive(s):
        rims[s][0].wait_recv()
        rims[s][blocks + 1].start()
        for copy in own_copies[s]:
            copy.wait()
        for copy in rims[s][1:]:
            copy.wait_recv()

    arrive(0)

    def stage_one(t, carry):
        waves = []
        for q in range(PAIR):
            p = t * PAIR + q
            patch = cut(p, 0)
            first_cut[p, 0], first_cut[p, 1] = patch
            waves += [times(w, patch) for w in waves_of(probe_rolled, p)]
        waves = two_sided(tables, *spread, waves)
        for q in range(PAIR):
            store_waves(wave_mid, t * PAIR + q, waves[q * modes : (q + 1) * modes])
        return carry

    lax.fori_loop(0, cap // PAIR, stage_one, 0)

    arrive(1)

    own_count = count_ref[g, m]

    def stage_two(t, carry):
        patches, mids, waves = [], [], []
        for q in range(PAIR):
            p = t * PAIR + q
            patches.append(cut(p, 1))
            mids.append(waves_of(wave_mid, p))
            waves += [times(w, patches[q]) for w in mids[q]]
        far = two_sided(tables, *fourier, waves)
        waves = []
        for q in range(PAIR):
            p = t * PAIR + q
            intensity = None
            for w in far[q * modes : (q + 1) * modes]:
                power = w[0] * w[0] + w[1] * w[1]
                intensity = power if intensity is None else intensity + power
            valid = jnp.where(p < own_count, 2.0, 0.0).astype(F32)
            slope = valid * (1.0 - measured_ref[p] * lax.rsqrt(intensity + 1.0))
            waves += [(w[0] * slope, w[1] * slope) for w in far[q * modes : (q + 1) * modes]]
        back = two_sided(tables, *fourier_conj, waves)
        for q in range(PAIR):
            p = t * PAIR + q
            own = back[q * modes : (q + 1) * modes]
            grad = None
            for mid, w in zip(mids[q], own):
                term = conj_times(mid, w)
                grad = term if grad is None else plus(grad, term)
            store_pieces(1, p, grad)
            store_waves(wave_back, p, [conj_times(patches[q], w) for w in own])
        return carry

    lax.fori_loop(0, cap // PAIR, stage_two, 0)

    homes = []
    for s in range(2):
        homes.append(
            (
                remote(rim_row.at[s, :, :, rest], land_row.at[s, :, :, rest], out_send.at[s, 0], out_recv.at[s, 0], down),
                remote(rim_row.at[s, :, :, low], land_corner.at[s], out_send.at[s, 1], out_recv.at[s, 1], right),
                remote(rim_col.at[s], land_col.at[s], out_send.at[s, 2], out_recv.at[s, 2], right),
                remote(rim_row.at[s, :, :, edge], land_row.at[s, :, :, edge], out_send.at[s, 3], out_recv.at[s, 3], down),
            )
        )

    def send_corner(s):
        homes[s][1].wait_recv()
        rim_row[s, :, :, edge] += land_corner[s]
        homes[s][3].start()

    assemble_many(1, blocks - 1, lambda s, t: assemble_low(s, t + 1))
    homes[1][0].start()
    assemble_low(1, blocks)
    homes[1][1].start()
    assemble_low(1, 0)
    assemble_many(1, blocks, assemble_wide)
    homes[1][2].start()

    probe_acc[...] = jnp.zeros(probe_acc.shape, F32)

    def stage_three(t, carry):
        waves = []
        for q in range(PAIR):
            waves += waves_of(wave_back, t * PAIR + q)
        waves = two_sided(tables, *spread_conj, waves)
        turned_back = [[] for _ in range(PAIR * modes)]
        for q in range(PAIR):
            p = t * PAIR + q
            patch = (first_cut[p, 0], first_cut[p, 1])
            grad = None
            for k, (probe, w) in enumerate(zip(waves_of(probe_rolled, p), waves[q * modes : (q + 1) * modes])):
                term = conj_times(probe, w)
                grad = term if grad is None else plus(grad, term)
                turned = turned_back[q * modes + k]
                for plane, x in enumerate(conj_times(patch, w)):
                    turned.append(x)
            store_pieces(0, p, grad)
        for k in range(modes):
            for plane in range(2):
                total = None
                for q in range(PAIR):
                    _, _, cs = place(t * PAIR + q)
                    x = pltpu.roll(turned_back[q * modes + k][plane], lax.rem(size - cs, size), axis=1)
                    total = x if total is None else total + x
                probe_acc[pl.ds((2 * k + plane) * size, size), :] += total
        return carry

    lax.fori_loop(0, cap // PAIR, stage_three, 0)

    rows = probe_acc.shape[0]
    half = rows // 2
    pair = remote(probe_acc.at[spot_of((1 - core) * half, half)], land_pair, pair_sem.at[0], pair_sem.at[1], partner)
    pair.start()
    assemble_many(0, blocks + 1, assemble_low)
    homes[0][1].start()
    send_corner(1)
    pair.wait_recv()
    land_pair[...] += probe_acc[spot_of(core * half, half)]

    sent = [pair]

    def added(land, n, copies):
        for copy in copies:
            copy.wait_recv()
        sent.extend(copies)
        total = land[0]
        for t in range(1, n):
            total = total + land[t]
        return total

    part = half // chips
    copies = []
    for d in range(1, chips):
        other = lax.rem(chip + d, chips)
        to = (g, 2 * other + core)
        copies.append(remote(land_pair.at[spot_of(other * part, part)], land_plane.at[chip], plane_send.at[d], plane_recv.at[d], to))
        copies[-1].start()
    land_plane[chip] = land_pair[spot_of(chip * part, part)]
    assemble_many(0, blocks, assemble_wide)
    homes[0][2].start()
    part_sum[...] = added(land_plane, chips, copies)
    land_z[g] = part_sum[...]
    copies = []
    for d in range(1, ng):
        to = (lax.rem(g + d, ng), m)
        copies.append(remote(part_sum, land_z.at[g], z_send.at[d], z_recv.at[d], to))
        copies[-1].start()
    homes[0][0].start()
    send_corner(0)
    assemble_many(1, blocks * blocks, assemble_own)
    assemble_many(0, blocks * blocks, assemble_own)
    positions = jnp.sum(counts_ref[...].astype(F32), keepdims=True)
    spot = spot_of(core * half + chip * part, part)
    probe_sum[spot] = added(land_z, ng, copies) / jnp.sqrt(positions)
    copies = []
    for d in range(1, chips):
        to = (g, 2 * lax.rem(chip + d, chips) + core)
        copies.append(remote(probe_sum.at[spot], probe_sum.at[spot], back_send.at[d], back_recv.at[d], to))
        copies[-1].start()

    def finish(s):
        for n in (0, 2, 3):
            homes[s][n].wait_recv()
        grad_ref[s, :, pl.ds(0, size), wide] += land_row[s]
        grad_ref[s, :, wide, pl.ds(0, size)] += land_col[s]

    finish(1)
    for copy in copies:
        copy.wait_recv()
    sent.extend(copies)
    mine = spot_of(core * half, half)
    share = remote(probe_sum.at[mine], probe_sum.at[mine], pair_sem.at[2], pair_sem.at[3], partner)
    share.start()
    finish(0)
    share.wait_recv()
    for plane in range(2 * modes):
        probe_grad_ref[plane] = probe_sum[pl.ds(plane * size, size), :]

    for s in range(2):
        for copy in [*rims[s], *homes[s]]:
            copy.wait_send()
    for copy in [*sent, share]:
        copy.wait_send()


def per_device(object_tiles, probe_modes, measured, slot_offset, slot_count):
    ng, nm = lax.axis_size("group"), lax.axis_size("member")
    tile = object_tiles.shape[-1]
    size = probe_modes.shape[-1]
    cap = measured.shape[2]
    planes = 2 * probe_modes.shape[0]
    ext = tile + size
    blocks = tile // size
    chips = nm // 2
    rows = planes * size
    step = rows // 2 // chips
    tables = jnp.asarray(make_tables(size))
    vmem = pl.BlockSpec(memory_space=pltpu.VMEM)
    hbm = pl.BlockSpec(memory_space=pltpu.HBM)
    dma = pltpu.SemaphoreType.DMA

    def body(*refs):
        kernel(ng, nm, tile, size, cap, *refs)

    grad, probe_grad = pl.pallas_call(
        body,
        out_shape=(
            pltpu.VMEM(object_tiles.shape, F32),
            pltpu.VMEM((planes, size, size), F32),
        ),
        in_specs=[hbm] * 6,
        out_specs=(vmem, vmem),
        scratch_shapes=[
            pltpu.SMEM((1, 1, 2, cap), jnp.int32),
            pltpu.SMEM(slot_count.shape, jnp.int32),
            pltpu.VMEM(slot_count.shape, jnp.int32),
            pltpu.VMEM((planes, size, size), F32),
            pltpu.VMEM((cap, size, size), F32),
            pltpu.VMEM(tables.shape, BF16),
            dma((6,)),
            pltpu.VMEM((blocks + 1, 2, ext, size), F32),
            pltpu.VMEM((blocks + 1, 2, ext, size), F32),
            pltpu.VMEM((2, 2, size, ext), F32),
            pltpu.VMEM((2, 2, tile, size), F32),
            pltpu.VMEM((2, 2, size, tile), F32),
            pltpu.VMEM((2, 2, tile, size), F32),
            pltpu.VMEM((2, 2, size, size), F32),
            pltpu.VMEM((cap, planes, size, size), F32),
            pltpu.VMEM((cap, 2, size, size), F32),
            pltpu.VMEM((cap, planes, size, size), F32),
            pltpu.VMEM((cap, planes, size, size), F32),
            pltpu.VMEM((2, cap, 2, 2, 3 * size, size), F32),
            pltpu.VMEM((rows, size), F32),
            pltpu.VMEM((rows // 2, size), F32),
            pltpu.VMEM((chips, step, size), F32),
            pltpu.VMEM((step, size), F32),
            pltpu.VMEM((ng, step, size), F32),
            pltpu.VMEM((rows, size), F32),
            dma((2, blocks + 2)),
            dma((2, blocks + 2)),
            dma((2, blocks)),
            dma((2, 4)),
            dma((2, 4)),
            dma((4,)),
            dma((chips,)),
            dma((chips,)),
            dma((ng,)),
            dma((ng,)),
            dma((chips,)),
            dma((chips,)),
        ],
        compiler_params=pltpu.CompilerParams(
            collective_id=0, has_side_effects=True, vmem_limit_bytes=48 * 1024 * 1024
        ),
    )(
        *(
            pltpu.with_memory_space_constraint(x, pltpu.HBM)
            for x in (
                jnp.swapaxes(slot_offset, 2, 3),
                slot_count,
                object_tiles,
                probe_modes.reshape(planes, size, size),
                measured.reshape(cap, size, size),
                tables,
            )
        ),
    )
    return grad, probe_grad.reshape(probe_modes.shape)


def solution(mesh):
    placed = (
        P(None, None, "group", "member"),
        P(),
        P("group", "member", None, None, None),
        P("group", "member", None, None),
        P(),
    )
    return jax.shard_map(
        per_device,
        mesh=mesh,
        in_specs=placed,
        out_specs=(P(None, None, "group", "member"), P()),
        check_vma=False,
    )
```

```python
import math

import jax
import jax.numpy as jnp
import ml_dtypes
import numpy as np
from jax import lax
from jax.experimental import pallas as pl
from jax.experimental.pallas import tpu as pltpu
from jax.sharding import PartitionSpec as P

MESH = pl.DeviceIdType.MESH
F32 = jnp.float32
BF16 = jnp.bfloat16
FRESNEL_RATE = 0.5
PAIR = 4


def make_tables(size):
    freq = np.arange(size)
    fourier = np.exp(-2j * np.pi * (np.outer(freq, freq) % size) / size) / math.sqrt(size)
    signed = np.where(freq >= size // 2, freq - size, freq).astype(np.float64)
    kernel = np.exp(-1j * np.pi * FRESNEL_RATE * signed**2 / size)
    spread = fourier.conj() @ (kernel[:, None] * fourier)
    spread = 0.5 * (spread + spread.T)
    forms = []
    for matrix in (fourier, spread):
        real, imag = matrix.real, matrix.imag
        forms.append(np.block([[real, -imag], [imag, real]]))
        forms.append(np.block([[real, imag], [-imag, real]]))
    exact = np.stack(forms)
    high = exact.astype(ml_dtypes.bfloat16)
    low = (exact - high.astype(np.float64)).astype(ml_dtypes.bfloat16)
    return np.stack([high, low], axis=1)


def split(x):
    high = x.astype(BF16)
    return high, (x - high.astype(F32)).astype(BF16)


def dot(a, b):
    return jnp.dot(a, b, preferred_element_type=F32)


def two_sided(tables, left, right, waves):
    size = waves[0][0].shape[0]
    x = jnp.concatenate(
        [jnp.concatenate([w[0] for w in waves], axis=1), jnp.concatenate([w[1] for w in waves], axis=1)], axis=0
    )
    high, low = split(x)
    t_high, t_low = tables[left, 0], tables[left, 1]
    t = dot(jnp.concatenate([t_high, t_high, t_low], axis=1), jnp.concatenate([high, low, high], axis=0))
    rows = []
    for j in range(len(waves)):
        cols = slice(j * size, (j + 1) * size)
        rows.append(jnp.concatenate([t[:size, cols], t[size:, cols]], axis=1))
    high, low = split(jnp.concatenate(rows, axis=0))
    t_high, t_low = tables[right, 0], tables[right, 1]
    y = dot(jnp.concatenate([high, low, high], axis=1), jnp.concatenate([t_high, t_high, t_low], axis=0))
    return [(y[j * size : (j + 1) * size, :size], y[j * size : (j + 1) * size, size:]) for j in range(len(waves))]


def times(a, b):
    return a[0] * b[0] - a[1] * b[1], a[0] * b[1] + a[1] * b[0]


def conj_times(a, b):
    return a[0] * b[0] + a[1] * b[1], a[0] * b[1] - a[1] * b[0]


def plus(a, b):
    return a[0] + b[0], a[1] + b[1]


class Many:
    def __init__(self, copies):
        self.copies = list(copies)

    def start(self):
        for copy in self.copies:
            copy.start()

    def wait_recv(self):
        for copy in self.copies:
            copy.wait_recv()

    def wait_send(self):
        for copy in self.copies:
            copy.wait_send()


def kernel(
    ng,
    nm,
    tile,
    size,
    cap,
    offset_hbm,
    counts_hbm,
    object_ref,
    probe_hbm,
    measured_hbm,
    tables_hbm,
    grad_ref,
    probe_grad_ref,
    offset_ref,
    count_ref,
    counts_ref,
    probe_ref,
    measured_ref,
    tables,
    load_sem,
    ext_a,
    ext_b,
    rim_row,
    rim_col,
    land_row,
    land_col,
    land_corner,
    probe_rolled,
    first_cut,
    wave_mid,
    wave_back,
    pieces,
    probe_acc,
    land_pair,
    land_plane,
    part_sum,
    land_z,
    probe_sum,
    in_send,
    in_recv,
    own_sem,
    out_send,
    out_recv,
    pair_sem,
    plane_send,
    plane_recv,
    z_send,
    z_recv,
    back_send,
    back_recv,
):
    g, m = lax.axis_index("group"), lax.axis_index("member")
    left, right = (g, lax.rem(m + nm - 1, nm)), (g, lax.rem(m + 1, nm))
    up, down = (lax.rem(g + ng - 1, ng), m), (lax.rem(g + 1, ng), m)
    core, chip = lax.rem(m, 2), m // 2
    chips = nm // 2
    partner = (g, m + 1 - 2 * core)
    blocks = tile // size
    modes = probe_ref.shape[0] // 2
    ext = (ext_a, ext_b)

    def spot_of(start, length):
        return pl.ds(pl.multiple_of(start, 8), length)

    def remote(src, dst, send, recv, device):
        return pltpu.make_async_remote_copy(
            src_ref=src, dst_ref=dst, send_sem=send, recv_sem=recv, device_id=device, device_id_type=MESH
        )

    barrier = pltpu.get_barrier_semaphore()
    greeted = [up, down, left, right]
    greeted += [(g, 2 * lax.rem(chip + d, chips) + core) for d in range(1, chips)]
    greeted += [(lax.rem(g + d, ng), m) for d in range(2, ng - 1)]
    for device in greeted:
        pl.semaphore_signal(barrier, inc=1, device_id=device, device_id_type=MESH)
    pl.semaphore_wait(barrier, len(greeted))

    low, wide, edge = pl.ds(tile, size), pl.ds(0, tile), pl.ds(0, size)
    rest = pl.ds(size, tile - size)
    rims = []
    for s in range(2):
        rims.append(
            [
                remote(object_ref.at[s, :, edge, pl.ds(j * size, size)], ext[s].at[j, :, low], in_send.at[s, j], in_recv.at[s, j], up)
                for j in range(blocks)
            ]
            + [
                remote(object_ref.at[s, :, :, edge], ext[s].at[blocks, :, wide], in_send.at[s, blocks], in_recv.at[s, blocks], left),
                remote(ext[s].at[0, :, low], ext[s].at[blocks, :, low], in_send.at[s, blocks + 1], in_recv.at[s, blocks + 1], left),
            ]
        )
        for copy in rims[s][: blocks + 1]:
            copy.start()

    own_copies = [
        [
            pltpu.make_async_copy(object_ref.at[s, :, :, pl.ds(j * size, size)], ext[s].at[j, :, wide], own_sem.at[s, j])
            for j in range(blocks)
        ]
        for s in range(2)
    ]
    loads = [
        pltpu.make_async_copy(src, dst, load_sem.at[n])
        for n, (src, dst) in enumerate(
            (
                (offset_hbm, offset_ref),
                (probe_hbm, probe_ref),
                (tables_hbm, tables),
                (measured_hbm, measured_ref),
                (counts_hbm, count_ref),
                (counts_hbm, counts_ref),
            )
        )
    ]
    for copy in loads + own_copies[0] + own_copies[1]:
        copy.start()

    def place(p):
        row, col = offset_ref[0, 0, 0, p], offset_ref[0, 0, 1, p]
        return row, col // size, lax.rem(col, size)

    for copy in loads:
        copy.wait()

    def roll_probe(p, carry):
        _, _, cs = place(p)
        for plane in range(2 * modes):
            probe_rolled[p, plane] = pltpu.roll(probe_ref[plane], cs, axis=1)
        return carry

    lax.fori_loop(0, cap, roll_probe, 0)

    def from_start(cs):
        return lax.broadcasted_iota(jnp.int32, (size, size), 1) >= cs

    def cut(p, s):
        row, bj, cs = place(p)
        inside = from_start(cs)
        rows = pl.ds(row, size)
        return tuple(jnp.where(inside, ext[s][bj, plane, rows], ext[s][bj + 1, plane, rows]) for plane in range(2))

    def waves_of(ref, p):
        return [(ref[p, 2 * k], ref[p, 2 * k + 1]) for k in range(modes)]

    def store_waves(ref, p, waves):
        for k in range(modes):
            ref[p, 2 * k] = waves[k][0]
            ref[p, 2 * k + 1] = waves[k][1]

    def store_pieces(s, p, grad):
        _, _, cs = place(p)
        inside = from_start(cs)
        for plane in range(2):
            pieces[s, p, 0, plane, pl.ds(size, size)] = jnp.where(inside, grad[plane], 0.0)
            pieces[s, p, 1, plane, pl.ds(size, size)] = jnp.where(inside, 0.0, grad[plane])

    def clear_pieces(p, carry):
        for n in (0, 2):
            for s in range(2):
                pieces[s, p, :, :, pl.ds(n * size, size)] = jnp.zeros((2, 2, size, size), F32)
        return carry

    lax.fori_loop(0, cap, clear_pieces, 0)

    def assemble(s, i, j):
        total = None
        for p in range(cap):
            row, bj, _ = place(p)
            b = j - bj
            inside = (b >= 0) & (b <= 1)
            start = jnp.where(inside, jnp.clip((i + 1) * size - row, 0, 2 * size), 0)
            part = pieces[s, p, jnp.where(inside, b, 0), :, pl.ds(start, size)]
            total = part if total is None else total + part
        return total

    def span(t):
        return pl.ds(pl.multiple_of(t * size, size), size)

    def assemble_low(s, j):
        rim_row[s, :, :, span(j)] = assemble(s, blocks, j)

    def assemble_wide(s, i):
        rim_col[s, :, span(i)] = assemble(s, i, blocks)

    def assemble_own(s, t):
        i, j = t // blocks, lax.rem(t, blocks)
        grad_ref[s, :, span(i), span(j)] = assemble(s, i, j)

    def assemble_many(s, n, one):
        def step(t, carry):
            one(s, t)
            return carry

        lax.fori_loop(0, n, step, 0)

    fourier, fourier_conj, spread, spread_conj = (0, 1), (1, 0), (2, 3), (3, 2)

    def arrive(s):
        rims[s][0].wait_recv()
        rims[s][blocks + 1].start()
        for copy in own_copies[s]:
            copy.wait()
        for copy in rims[s][1:]:
            copy.wait_recv()

    arrive(0)

    def stage_one(t, carry):
        waves = []
        for q in range(PAIR):
            p = t * PAIR + q
            patch = cut(p, 0)
            first_cut[p, 0], first_cut[p, 1] = patch
            waves += [times(w, patch) for w in waves_of(probe_rolled, p)]
        waves = two_sided(tables, *spread, waves)
        for q in range(PAIR):
            store_waves(wave_mid, t * PAIR + q, waves[q * modes : (q + 1) * modes])
        return carry

    lax.fori_loop(0, cap // PAIR, stage_one, 0)

    arrive(1)

    own_count = count_ref[g, m]

    def stage_two(t, carry):
        patches, mids, waves = [], [], []
        for q in range(PAIR):
            p = t * PAIR + q
            patches.append(cut(p, 1))
            mids.append(waves_of(wave_mid, p))
            waves += [times(w, patches[q]) for w in mids[q]]
        far = two_sided(tables, *fourier, waves)
        waves = []
        for q in range(PAIR):
            p = t * PAIR + q
            intensity = None
            for w in far[q * modes : (q + 1) * modes]:
                power = w[0] * w[0] + w[1] * w[1]
                intensity = power if intensity is None else intensity + power
            valid = jnp.where(p < own_count, 2.0, 0.0).astype(F32)
            slope = valid * (1.0 - measured_ref[p] * lax.rsqrt(intensity + 1.0))
            waves += [(w[0] * slope, w[1] * slope) for w in far[q * modes : (q + 1) * modes]]
        back = two_sided(tables, *fourier_conj, waves)
        for q in range(PAIR):
            p = t * PAIR + q
            own = back[q * modes : (q + 1) * modes]
            grad = None
            for mid, w in zip(mids[q], own):
                term = conj_times(mid, w)
                grad = term if grad is None else plus(grad, term)
            store_pieces(1, p, grad)
            store_waves(wave_back, p, [conj_times(patches[q], w) for w in own])
        return carry

    lax.fori_loop(0, cap // PAIR, stage_two, 0)

    homes = []
    for s in range(2):
        homes.append(
            (
                Many(
                    remote(rim_row.at[s, :, :, part], land_row.at[s, :, :, part], out_send.at[s, 4 + j], out_recv.at[s, 4 + j], down)
                    for j, part in ((j, pl.ds((j + 1) * size, size)) for j in range(blocks - 1))
                ),
                remote(rim_row.at[s, :, :, low], land_corner.at[s], out_send.at[s, 1], out_recv.at[s, 1], right),
                remote(rim_col.at[s], land_col.at[s], out_send.at[s, 2], out_recv.at[s, 2], right),
                remote(rim_row.at[s, :, :, edge], land_row.at[s, :, :, edge], out_send.at[s, 3], out_recv.at[s, 3], down),
            )
        )

    def send_corner(s):
        homes[s][1].wait_recv()
        rim_row[s, :, :, edge] += land_corner[s]
        homes[s][3].start()

    assemble_low(1, blocks)
    homes[1][1].start()
    assemble_many(1, blocks, assemble_wide)
    homes[1][2].start()
    assemble_many(1, blocks - 1, lambda s, t: assemble_low(s, t + 1))
    homes[1][0].start()
    assemble_low(1, 0)

    probe_acc[...] = jnp.zeros(probe_acc.shape, F32)

    def stage_three(t, carry):
        waves = []
        for q in range(PAIR):
            waves += waves_of(wave_back, t * PAIR + q)
        waves = two_sided(tables, *spread_conj, waves)
        turned_back = [[] for _ in range(PAIR * modes)]
        for q in range(PAIR):
            p = t * PAIR + q
            patch = (first_cut[p, 0], first_cut[p, 1])
            grad = None
            for k, (probe, w) in enumerate(zip(waves_of(probe_rolled, p), waves[q * modes : (q + 1) * modes])):
                term = conj_times(probe, w)
                grad = term if grad is None else plus(grad, term)
                turned = turned_back[q * modes + k]
                for plane, x in enumerate(conj_times(patch, w)):
                    turned.append(x)
            store_pieces(0, p, grad)
        for k in range(modes):
            for plane in range(2):
                total = None
                for q in range(PAIR):
                    _, _, cs = place(t * PAIR + q)
                    x = pltpu.roll(turned_back[q * modes + k][plane], lax.rem(size - cs, size), axis=1)
                    total = x if total is None else total + x
                probe_acc[pl.ds((2 * k + plane) * size, size), :] += total
        return carry

    lax.fori_loop(0, cap // PAIR, stage_three, 0)

    def finish(s):
        homes[s][2].wait_recv()
        grad_ref[s, :, wide, edge] += land_col[s]
        homes[s][0].wait_recv()
        grad_ref[s, :, edge, rest] += land_row[s, :, :, rest]
        homes[s][3].wait_recv()
        grad_ref[s, :, edge, edge] += land_row[s, :, :, edge]

    rows = probe_acc.shape[0]
    half = rows // 2
    pair = remote(probe_acc.at[spot_of((1 - core) * half, half)], land_pair, pair_sem.at[0], pair_sem.at[1], partner)
    pair.start()
    assemble_low(0, blocks)
    homes[0][1].start()
    assemble_many(0, blocks, assemble_low)
    send_corner(1)
    pair.wait_recv()
    land_pair[...] += probe_acc[spot_of(core * half, half)]

    sent = [pair]

    def added(land, n, copies):
        for copy in copies:
            copy.wait_recv()
        sent.extend(copies)
        total = land[0]
        for t in range(1, n):
            total = total + land[t]
        return total

    part = half // chips
    for copy in homes[0][0].copies[:1]:
        copy.start()
    copies = []
    for d in range(1, chips):
        other = lax.rem(chip + d, chips)
        to = (g, 2 * other + core)
        copies.append(remote(land_pair.at[spot_of(other * part, part)], land_plane.at[chip], plane_send.at[d], plane_recv.at[d], to))
        copies[-1].start()
    land_plane[chip] = land_pair[spot_of(chip * part, part)]
    assemble_many(0, blocks, assemble_wide)
    part_sum[...] = added(land_plane, chips, copies)
    land_z[g] = part_sum[...]
    copies = []
    for d in range(1, ng):
        to = (lax.rem(g + d, ng), m)
        copies.append(remote(part_sum, land_z.at[g], z_send.at[d], z_recv.at[d], to))
        copies[-1].start()
    for copy in homes[0][0].copies[1:]:
        copy.start()
    homes[0][2].start()
    send_corner(0)
    assemble_many(1, blocks * blocks, assemble_own)
    assemble_many(0, blocks * blocks, assemble_own)
    finish(1)
    positions = jnp.sum(counts_ref[...].astype(F32), keepdims=True)
    spot = spot_of(core * half + chip * part, part)
    probe_sum[spot] = added(land_z, ng, copies) / jnp.sqrt(positions)
    copies = []
    for d in range(1, chips):
        to = (g, 2 * lax.rem(chip + d, chips) + core)
        copies.append(remote(probe_sum.at[spot], probe_sum.at[spot], back_send.at[d], back_recv.at[d], to))
        copies[-1].start()

    for copy in copies:
        copy.wait_recv()
    sent.extend(copies)
    mine = spot_of(core * half, half)
    share = remote(probe_sum.at[mine], probe_sum.at[mine], pair_sem.at[2], pair_sem.at[3], partner)
    share.start()
    finish(0)
    share.wait_recv()
    for plane in range(2 * modes):
        probe_grad_ref[plane] = probe_sum[pl.ds(plane * size, size), :]

    for s in range(2):
        for copy in [*rims[s], *homes[s]]:
            copy.wait_send()
    for copy in [*sent, share]:
        copy.wait_send()


def per_device(object_tiles, probe_modes, measured, slot_offset, slot_count):
    ng, nm = lax.axis_size("group"), lax.axis_size("member")
    tile = object_tiles.shape[-1]
    size = probe_modes.shape[-1]
    cap = measured.shape[2]
    planes = 2 * probe_modes.shape[0]
    ext = tile + size
    blocks = tile // size
    chips = nm // 2
    rows = planes * size
    step = rows // 2 // chips
    tables = jnp.asarray(make_tables(size))
    vmem = pl.BlockSpec(memory_space=pltpu.VMEM)
    hbm = pl.BlockSpec(memory_space=pltpu.HBM)
    dma = pltpu.SemaphoreType.DMA

    def body(*refs):
        kernel(ng, nm, tile, size, cap, *refs)

    grad, probe_grad = pl.pallas_call(
        body,
        out_shape=(
            pltpu.VMEM(object_tiles.shape, F32),
            pltpu.VMEM((planes, size, size), F32),
        ),
        in_specs=[hbm] * 6,
        out_specs=(vmem, vmem),
        scratch_shapes=[
            pltpu.SMEM((1, 1, 2, cap), jnp.int32),
            pltpu.SMEM(slot_count.shape, jnp.int32),
            pltpu.VMEM(slot_count.shape, jnp.int32),
            pltpu.VMEM((planes, size, size), F32),
            pltpu.VMEM((cap, size, size), F32),
            pltpu.VMEM(tables.shape, BF16),
            dma((6,)),
            pltpu.VMEM((blocks + 1, 2, ext, size), F32),
            pltpu.VMEM((blocks + 1, 2, ext, size), F32),
            pltpu.VMEM((2, 2, size, ext), F32),
            pltpu.VMEM((2, 2, tile, size), F32),
            pltpu.VMEM((2, 2, size, tile), F32),
            pltpu.VMEM((2, 2, tile, size), F32),
            pltpu.VMEM((2, 2, size, size), F32),
            pltpu.VMEM((cap, planes, size, size), F32),
            pltpu.VMEM((cap, 2, size, size), F32),
            pltpu.VMEM((cap, planes, size, size), F32),
            pltpu.VMEM((cap, planes, size, size), F32),
            pltpu.VMEM((2, cap, 2, 2, 3 * size, size), F32),
            pltpu.VMEM((rows, size), F32),
            pltpu.VMEM((rows // 2, size), F32),
            pltpu.VMEM((chips, step, size), F32),
            pltpu.VMEM((step, size), F32),
            pltpu.VMEM((ng, step, size), F32),
            pltpu.VMEM((rows, size), F32),
            dma((2, blocks + 2)),
            dma((2, blocks + 2)),
            dma((2, blocks)),
            dma((2, 3 + blocks)),
            dma((2, 3 + blocks)),
            dma((4,)),
            dma((chips,)),
            dma((chips,)),
            dma((ng,)),
            dma((ng,)),
            dma((chips,)),
            dma((chips,)),
        ],
        compiler_params=pltpu.CompilerParams(
            collective_id=0, has_side_effects=True, vmem_limit_bytes=48 * 1024 * 1024
        ),
    )(
        *(
            pltpu.with_memory_space_constraint(x, pltpu.HBM)
            for x in (
                jnp.swapaxes(slot_offset, 2, 3),
                slot_count,
                object_tiles,
                probe_modes.reshape(planes, size, size),
                measured.reshape(cap, size, size),
                tables,
            )
        ),
    )
    return grad, probe_grad.reshape(probe_modes.shape)


def solution(mesh):
    placed = (
        P(None, None, "group", "member"),
        P(),
        P("group", "member", None, None, None),
        P("group", "member", None, None),
        P(),
    )
    return jax.shard_map(
        per_device,
        mesh=mesh,
        in_specs=placed,
        out_specs=(P(None, None, "group", "member"), P()),
        check_vma=False,
    )
```

```python
import math

import jax
import jax.numpy as jnp
import ml_dtypes
import numpy as np
from jax import lax
from jax.experimental import pallas as pl
from jax.experimental.pallas import tpu as pltpu
from jax.sharding import PartitionSpec as P

MESH = pl.DeviceIdType.MESH
F32 = jnp.float32
BF16 = jnp.bfloat16
FRESNEL_RATE = 0.5
PAIR = 4


def make_tables(size):
    freq = np.arange(size)
    fourier = np.exp(-2j * np.pi * (np.outer(freq, freq) % size) / size) / math.sqrt(size)
    signed = np.where(freq >= size // 2, freq - size, freq).astype(np.float64)
    kernel = np.exp(-1j * np.pi * FRESNEL_RATE * signed**2 / size)
    spread = fourier.conj() @ (kernel[:, None] * fourier)
    spread = 0.5 * (spread + spread.T)
    forms = []
    for matrix in (fourier, spread):
        real, imag = matrix.real, matrix.imag
        forms.append(np.block([[real, -imag], [imag, real]]))
        forms.append(np.block([[real, imag], [-imag, real]]))
    exact = np.stack(forms)
    high = exact.astype(ml_dtypes.bfloat16)
    low = (exact - high.astype(np.float64)).astype(ml_dtypes.bfloat16)
    return np.stack([high, low], axis=1)


def split(x):
    high = x.astype(BF16)
    return high, (x - high.astype(F32)).astype(BF16)


def dot(a, b):
    return jnp.dot(a, b, preferred_element_type=F32)


def two_sided(tables, left, right, waves):
    size = waves[0][0].shape[0]
    x = jnp.concatenate(
        [jnp.concatenate([w[0] for w in waves], axis=1), jnp.concatenate([w[1] for w in waves], axis=1)], axis=0
    )
    high, low = split(x)
    t_high, t_low = tables[left, 0], tables[left, 1]
    t = dot(jnp.concatenate([t_high, t_high, t_low], axis=1), jnp.concatenate([high, low, high], axis=0))
    rows = []
    for j in range(len(waves)):
        cols = slice(j * size, (j + 1) * size)
        rows.append(jnp.concatenate([t[:size, cols], t[size:, cols]], axis=1))
    high, low = split(jnp.concatenate(rows, axis=0))
    t_high, t_low = tables[right, 0], tables[right, 1]
    y = dot(jnp.concatenate([high, low, high], axis=1), jnp.concatenate([t_high, t_high, t_low], axis=0))
    return [(y[j * size : (j + 1) * size, :size], y[j * size : (j + 1) * size, size:]) for j in range(len(waves))]


def times(a, b):
    return a[0] * b[0] - a[1] * b[1], a[0] * b[1] + a[1] * b[0]


def conj_times(a, b):
    return a[0] * b[0] + a[1] * b[1], a[0] * b[1] - a[1] * b[0]


def plus(a, b):
    return a[0] + b[0], a[1] + b[1]


class Many:
    def __init__(self, copies):
        self.copies = list(copies)

    def __getitem__(self, key):
        return Many(self.copies[key])

    def start(self):
        for copy in self.copies:
            copy.start()

    def wait_recv(self):
        for copy in self.copies:
            copy.wait_recv()

    def wait_send(self):
        for copy in self.copies:
            copy.wait_send()


class Bounded:
    def __init__(self, copy, sends, takes):
        self.copy, self.sends, self.takes = copy, sends, takes

    def start(self):
        pl.when(self.sends)(self.copy.start)

    def wait_recv(self):
        pl.when(self.takes)(self.copy.wait_recv)

    def wait_send(self):
        pl.when(self.sends)(self.copy.wait_send)


def kernel(
    ng,
    nm,
    tile,
    size,
    cap,
    offset_hbm,
    counts_hbm,
    object_ref,
    probe_hbm,
    measured_hbm,
    tables_hbm,
    grad_ref,
    probe_grad_ref,
    offset_ref,
    count_ref,
    counts_ref,
    probe_ref,
    measured_ref,
    tables,
    load_sem,
    ext_a,
    ext_b,
    rim_row,
    rim_col,
    land_row,
    land_col,
    land_corner,
    probe_rolled,
    first_cut,
    wave_mid,
    wave_back,
    pieces,
    probe_acc,
    land_pair,
    land_plane,
    part_sum,
    land_z,
    probe_sum,
    in_send,
    in_recv,
    own_sem,
    out_send,
    out_recv,
    pair_sem,
    plane_send,
    plane_recv,
    z_send,
    z_recv,
    back_send,
    back_recv,
):
    g, m = lax.axis_index("group"), lax.axis_index("member")
    left, right = (g, lax.rem(m + nm - 1, nm)), (g, lax.rem(m + 1, nm))
    up, down = (lax.rem(g + ng - 1, ng), m), (lax.rem(g + 1, ng), m)
    core, chip = lax.rem(m, 2), m // 2
    chips = nm // 2
    partner = (g, m + 1 - 2 * core)
    blocks = tile // size
    modes = probe_ref.shape[0] // 2
    ext = (ext_a, ext_b)

    def spot_of(start, length):
        return pl.ds(pl.multiple_of(start, 8), length)

    def remote(src, dst, send, recv, device):
        return pltpu.make_async_remote_copy(
            src_ref=src, dst_ref=dst, send_sem=send, recv_sem=recv, device_id=device, device_id_type=MESH
        )

    barrier = pltpu.get_barrier_semaphore()
    greeted = [up, down, left, right]
    greeted += [(g, 2 * lax.rem(chip + d, chips) + core) for d in range(1, chips)]
    greeted += [(lax.rem(g + d, ng), m) for d in range(2, ng - 1)]
    for device in greeted:
        pl.semaphore_signal(barrier, inc=1, device_id=device, device_id_type=MESH)
    pl.semaphore_wait(barrier, len(greeted))

    low, wide, edge = pl.ds(tile, size), pl.ds(0, tile), pl.ds(0, size)
    rest = pl.ds(size, tile - size)
    rims = []
    for s in range(2):
        rims.append(
            [
                remote(object_ref.at[s, :, edge, pl.ds(j * size, size)], ext[s].at[j, :, low], in_send.at[s, j], in_recv.at[s, j], up)
                for j in range(blocks)
            ]
            + [
                remote(object_ref.at[s, :, :, edge], ext[s].at[blocks, :, wide], in_send.at[s, blocks], in_recv.at[s, blocks], left),
                remote(ext[s].at[0, :, low], ext[s].at[blocks, :, low], in_send.at[s, blocks + 1], in_recv.at[s, blocks + 1], left),
            ]
        )
        for copy in rims[s][: blocks + 1]:
            copy.start()

    own_copies = [
        [
            pltpu.make_async_copy(object_ref.at[s, :, :, pl.ds(j * size, size)], ext[s].at[j, :, wide], own_sem.at[s, j])
            for j in range(blocks)
        ]
        for s in range(2)
    ]
    loads = [
        pltpu.make_async_copy(src, dst, load_sem.at[n])
        for n, (src, dst) in enumerate(
            (
                (offset_hbm, offset_ref),
                (probe_hbm, probe_ref),
                (tables_hbm, tables),
                (measured_hbm, measured_ref),
                (counts_hbm, count_ref),
                (counts_hbm, counts_ref),
            )
        )
    ]
    for copy in loads + own_copies[0] + own_copies[1]:
        copy.start()

    def place(p):
        row, col = offset_ref[0, 0, 0, p], offset_ref[0, 0, 1, p]
        return row, col // size, lax.rem(col, size)

    for copy in loads:
        copy.wait()

    def roll_probe(p, carry):
        _, _, cs = place(p)
        for plane in range(2 * modes):
            probe_rolled[p, plane] = pltpu.roll(probe_ref[plane], cs, axis=1)
        return carry

    lax.fori_loop(0, cap, roll_probe, 0)

    def from_start(cs):
        return lax.broadcasted_iota(jnp.int32, (size, size), 1) >= cs

    def cut(p, s):
        row, bj, cs = place(p)
        inside = from_start(cs)
        rows = pl.ds(row, size)
        return tuple(jnp.where(inside, ext[s][bj, plane, rows], ext[s][bj + 1, plane, rows]) for plane in range(2))

    def waves_of(ref, p):
        return [(ref[p, 2 * k], ref[p, 2 * k + 1]) for k in range(modes)]

    def store_waves(ref, p, waves):
        for k in range(modes):
            ref[p, 2 * k] = waves[k][0]
            ref[p, 2 * k + 1] = waves[k][1]

    def store_pieces(s, p, grad):
        _, _, cs = place(p)
        inside = from_start(cs)
        for plane in range(2):
            pieces[s, p, 0, plane, pl.ds(size, size)] = jnp.where(inside, grad[plane], 0.0)
            pieces[s, p, 1, plane, pl.ds(size, size)] = jnp.where(inside, 0.0, grad[plane])

    def clear_pieces(p, carry):
        for n in (0, 2):
            for s in range(2):
                pieces[s, p, :, :, pl.ds(n * size, size)] = jnp.zeros((2, 2, size, size), F32)
        return carry

    lax.fori_loop(0, cap, clear_pieces, 0)

    def assemble(s, i, j):
        total = None
        for p in range(cap):
            row, bj, _ = place(p)
            b = j - bj
            inside = (b >= 0) & (b <= 1)
            start = jnp.where(inside, jnp.clip((i + 1) * size - row, 0, 2 * size), 0)
            part = pieces[s, p, jnp.where(inside, b, 0), :, pl.ds(start, size)]
            total = part if total is None else total + part
        return total

    def span(t):
        return pl.ds(pl.multiple_of(t * size, size), size)

    def assemble_low(s, j):
        rim_row[s, :, :, span(j)] = assemble(s, blocks, j)

    def assemble_wide(s, i):
        rim_col[s, :, span(i)] = assemble(s, i, blocks)

    def assemble_own(s, t):
        i, j = t // blocks, lax.rem(t, blocks)
        grad_ref[s, :, span(i), span(j)] = assemble(s, i, j)

    def assemble_many(s, n, one):
        def step(t, carry):
            one(s, t)
            return carry

        lax.fori_loop(0, n, step, 0)

    fourier, fourier_conj, spread, spread_conj = (0, 1), (1, 0), (2, 3), (3, 2)

    def arrive(s):
        rims[s][0].wait_recv()
        rims[s][blocks + 1].start()
        for copy in own_copies[s]:
            copy.wait()
        for copy in rims[s][1:]:
            copy.wait_recv()

    arrive(0)

    def stage_one(t, carry):
        waves = []
        for q in range(PAIR):
            p = t * PAIR + q
            patch = cut(p, 0)
            first_cut[p, 0], first_cut[p, 1] = patch
            waves += [times(w, patch) for w in waves_of(probe_rolled, p)]
        waves = two_sided(tables, *spread, waves)
        for q in range(PAIR):
            store_waves(wave_mid, t * PAIR + q, waves[q * modes : (q + 1) * modes])
        return carry

    lax.fori_loop(0, cap // PAIR, stage_one, 0)

    arrive(1)

    own_count = count_ref[g, m]

    def stage_two(t, carry):
        patches, mids, waves = [], [], []
        for q in range(PAIR):
            p = t * PAIR + q
            patches.append(cut(p, 1))
            mids.append(waves_of(wave_mid, p))
            waves += [times(w, patches[q]) for w in mids[q]]
        far = two_sided(tables, *fourier, waves)
        waves = []
        for q in range(PAIR):
            p = t * PAIR + q
            intensity = None
            for w in far[q * modes : (q + 1) * modes]:
                power = w[0] * w[0] + w[1] * w[1]
                intensity = power if intensity is None else intensity + power
            valid = jnp.where(p < own_count, 2.0, 0.0).astype(F32)
            slope = valid * (1.0 - measured_ref[p] * lax.rsqrt(intensity + 1.0))
            waves += [(w[0] * slope, w[1] * slope) for w in far[q * modes : (q + 1) * modes]]
        back = two_sided(tables, *fourier_conj, waves)
        for q in range(PAIR):
            p = t * PAIR + q
            own = back[q * modes : (q + 1) * modes]
            grad = None
            for mid, w in zip(mids[q], own):
                term = conj_times(mid, w)
                grad = term if grad is None else plus(grad, term)
            store_pieces(1, p, grad)
            store_waves(wave_back, p, [conj_times(patches[q], w) for w in own])
        return carry

    lax.fori_loop(0, cap // PAIR, stage_two, 0)

    homes = []
    takes_rows, takes_cols = g > 0, m > 0

    def home_down(*args):
        return Bounded(remote(*args, down), g < ng - 1, takes_rows)

    def home_right(*args):
        return Bounded(remote(*args, right), m < nm - 1, takes_cols)

    for s in range(2):
        homes.append(
            (
                Many(
                    home_down(rim_row.at[s, :, :, part], land_row.at[s, :, :, part], out_send.at[s, 4 + j], out_recv.at[s, 4 + j])
                    for j, part in ((j, pl.ds((j + 1) * size, size)) for j in range(blocks - 1))
                ),
                home_right(rim_row.at[s, :, :, low], land_corner.at[s], out_send.at[s, 1], out_recv.at[s, 1]),
                Many(
                    home_right(rim_col.at[s, n], land_col.at[s, n], out_send.at[s, 2 * n], out_recv.at[s, 2 * n])
                    for n in range(2)
                ),
                home_down(rim_row.at[s, :, :, edge], land_row.at[s, :, :, edge], out_send.at[s, 3], out_recv.at[s, 3]),
            )
        )

    def send_corner(s):
        homes[s][1].wait_recv()

        @pl.when(takes_cols)
        def _():
            rim_row[s, :, :, edge] += land_corner[s]

        homes[s][3].start()

    assemble_low(1, blocks)
    homes[1][1].start()
    assemble_many(1, blocks, assemble_wide)
    homes[1][2].copies[0].start()
    assemble_many(1, blocks - 1, lambda s, t: assemble_low(s, t + 1))
    homes[1][0].start()
    assemble_low(1, 0)

    probe_acc[...] = jnp.zeros(probe_acc.shape, F32)

    def stage_three(t, carry):
        waves = []
        for q in range(PAIR):
            waves += waves_of(wave_back, t * PAIR + q)
        waves = two_sided(tables, *spread_conj, waves)
        turned_back = [[] for _ in range(PAIR * modes)]
        for q in range(PAIR):
            p = t * PAIR + q
            patch = (first_cut[p, 0], first_cut[p, 1])
            grad = None
            for k, (probe, w) in enumerate(zip(waves_of(probe_rolled, p), waves[q * modes : (q + 1) * modes])):
                term = conj_times(probe, w)
                grad = term if grad is None else plus(grad, term)
                turned = turned_back[q * modes + k]
                for plane, x in enumerate(conj_times(patch, w)):
                    turned.append(x)
            store_pieces(0, p, grad)
        for k in range(modes):
            for plane in range(2):
                total = None
                for q in range(PAIR):
                    _, _, cs = place(t * PAIR + q)
                    x = pltpu.roll(turned_back[q * modes + k][plane], lax.rem(size - cs, size), axis=1)
                    total = x if total is None else total + x
                probe_acc[pl.ds((2 * k + plane) * size, size), :] += total
        return carry

    lax.fori_loop(0, cap // PAIR, stage_three, 0)

    def finish(s):
        homes[s][2].wait_recv()

        @pl.when(takes_cols)
        def _():
            grad_ref[s, :, wide, edge] += land_col[s]

        homes[s][0].wait_recv()

        @pl.when(takes_rows)
        def _():
            grad_ref[s, :, edge, rest] += land_row[s, :, :, rest]

        homes[s][3].wait_recv()

        @pl.when(takes_rows)
        def _():
            grad_ref[s, :, edge, edge] += land_row[s, :, :, edge]

    rows = probe_acc.shape[0]
    half = rows // 2
    pair = remote(probe_acc.at[spot_of((1 - core) * half, half)], land_pair, pair_sem.at[0], pair_sem.at[1], partner)
    pair.start()
    assemble_low(0, blocks)
    homes[0][1].start()
    assemble_many(0, blocks, assemble_low)
    send_corner(1)
    pair.wait_recv()
    land_pair[...] += probe_acc[spot_of(core * half, half)]

    sent = [pair]

    def added(land, n, copies):
        for copy in copies:
            copy.wait_recv()
        sent.extend(copies)
        total = land[0]
        for t in range(1, n):
            total = total + land[t]
        return total

    part = half // chips
    copies = []
    for d in range(1, chips):
        other = lax.rem(chip + d, chips)
        to = (g, 2 * other + core)
        copies.append(remote(land_pair.at[spot_of(other * part, part)], land_plane.at[chip], plane_send.at[d], plane_recv.at[d], to))
        copies[-1].start()
    land_plane[chip] = land_pair[spot_of(chip * part, part)]
    assemble_many(0, blocks, assemble_wide)
    part_sum[...] = added(land_plane, chips, copies)
    land_z[g] = part_sum[...]
    copies = []
    for d in range(1, ng):
        to = (lax.rem(g + d, ng), m)
        copies.append(remote(part_sum, land_z.at[g], z_send.at[d], z_recv.at[d], to))
        copies[-1].start()
    homes[0][0].start()
    homes[1][2].copies[1].start()
    homes[0][2].copies[0].start()
    send_corner(0)
    assemble_many(1, blocks * blocks, assemble_own)
    assemble_many(0, blocks * blocks, assemble_own)
    finish(1)
    positions = jnp.sum(counts_ref[...].astype(F32), keepdims=True)
    spot = spot_of(core * half + chip * part, part)
    probe_sum[spot] = added(land_z, ng, copies) / jnp.sqrt(positions)
    copies = []
    for d in range(1, chips):
        to = (g, 2 * lax.rem(chip + d, chips) + core)
        copies.append(remote(probe_sum.at[spot], probe_sum.at[spot], back_send.at[d], back_recv.at[d], to))
        copies[-1].start()

    homes[0][2].copies[1].start()
    for copy in copies:
        copy.wait_recv()
    sent.extend(copies)
    mine = spot_of(core * half, half)
    share = remote(probe_sum.at[mine], probe_sum.at[mine], pair_sem.at[2], pair_sem.at[3], partner)
    share.start()
    finish(0)
    share.wait_recv()
    for plane in range(2 * modes):
        probe_grad_ref[plane] = probe_sum[pl.ds(plane * size, size), :]

    for s in range(2):
        for copy in [*rims[s], *homes[s]]:
            copy.wait_send()
    for copy in [*sent, share]:
        copy.wait_send()


def per_device(object_tiles, probe_modes, measured, slot_offset, slot_count):
    ng, nm = lax.axis_size("group"), lax.axis_size("member")
    tile = object_tiles.shape[-1]
    size = probe_modes.shape[-1]
    cap = measured.shape[2]
    planes = 2 * probe_modes.shape[0]
    ext = tile + size
    blocks = tile // size
    chips = nm // 2
    rows = planes * size
    step = rows // 2 // chips
    tables = jnp.asarray(make_tables(size))
    vmem = pl.BlockSpec(memory_space=pltpu.VMEM)
    hbm = pl.BlockSpec(memory_space=pltpu.HBM)
    dma = pltpu.SemaphoreType.DMA

    def body(*refs):
        kernel(ng, nm, tile, size, cap, *refs)

    grad, probe_grad = pl.pallas_call(
        body,
        out_shape=(
            pltpu.VMEM(object_tiles.shape, F32),
            pltpu.VMEM((planes, size, size), F32),
        ),
        in_specs=[hbm] * 6,
        out_specs=(vmem, vmem),
        scratch_shapes=[
            pltpu.SMEM((1, 1, 2, cap), jnp.int32),
            pltpu.SMEM(slot_count.shape, jnp.int32),
            pltpu.VMEM(slot_count.shape, jnp.int32),
            pltpu.VMEM((planes, size, size), F32),
            pltpu.VMEM((cap, size, size), F32),
            pltpu.VMEM(tables.shape, BF16),
            dma((6,)),
            pltpu.VMEM((blocks + 1, 2, ext, size), F32),
            pltpu.VMEM((blocks + 1, 2, ext, size), F32),
            pltpu.VMEM((2, 2, size, ext), F32),
            pltpu.VMEM((2, 2, tile, size), F32),
            pltpu.VMEM((2, 2, size, tile), F32),
            pltpu.VMEM((2, 2, tile, size), F32),
            pltpu.VMEM((2, 2, size, size), F32),
            pltpu.VMEM((cap, planes, size, size), F32),
            pltpu.VMEM((cap, 2, size, size), F32),
            pltpu.VMEM((cap, planes, size, size), F32),
            pltpu.VMEM((cap, planes, size, size), F32),
            pltpu.VMEM((2, cap, 2, 2, 3 * size, size), F32),
            pltpu.VMEM((rows, size), F32),
            pltpu.VMEM((rows // 2, size), F32),
            pltpu.VMEM((chips, step, size), F32),
            pltpu.VMEM((step, size), F32),
            pltpu.VMEM((ng, step, size), F32),
            pltpu.VMEM((rows, size), F32),
            dma((2, blocks + 2)),
            dma((2, blocks + 2)),
            dma((2, blocks)),
            dma((2, 3 + blocks)),
            dma((2, 3 + blocks)),
            dma((4,)),
            dma((chips,)),
            dma((chips,)),
            dma((ng,)),
            dma((ng,)),
            dma((chips,)),
            dma((chips,)),
        ],
        compiler_params=pltpu.CompilerParams(
            collective_id=0, has_side_effects=True, vmem_limit_bytes=48 * 1024 * 1024
        ),
    )(
        *(
            pltpu.with_memory_space_constraint(x, pltpu.HBM)
            for x in (
                jnp.swapaxes(slot_offset, 2, 3),
                slot_count,
                object_tiles,
                probe_modes.reshape(planes, size, size),
                measured.reshape(cap, size, size),
                tables,
            )
        ),
    )
    return grad, probe_grad.reshape(probe_modes.shape)


def solution(mesh):
    placed = (
        P(None, None, "group", "member"),
        P(),
        P("group", "member", None, None, None),
        P("group", "member", None, None),
        P(),
    )
    return jax.shard_map(
        per_device,
        mesh=mesh,
        in_specs=placed,
        out_specs=(P(None, None, "group", "member"), P()),
        check_vma=False,
    )
```

```python
import math

import jax
import jax.numpy as jnp
import ml_dtypes
import numpy as np
from jax import lax
from jax.experimental import pallas as pl
from jax.experimental.pallas import tpu as pltpu
from jax.sharding import PartitionSpec as P

MESH = pl.DeviceIdType.MESH
F32 = jnp.float32
BF16 = jnp.bfloat16
FRESNEL_RATE = 0.5
PAIR = 4


def make_tables(size):
    freq = np.arange(size)
    fourier = np.exp(-2j * np.pi * (np.outer(freq, freq) % size) / size) / math.sqrt(size)
    signed = np.where(freq >= size // 2, freq - size, freq).astype(np.float64)
    kernel = np.exp(-1j * np.pi * FRESNEL_RATE * signed**2 / size)
    spread = fourier.conj() @ (kernel[:, None] * fourier)
    spread = 0.5 * (spread + spread.T)
    forms = []
    for matrix in (fourier, spread):
        real, imag = matrix.real, matrix.imag
        forms.append(np.block([[real, -imag], [imag, real]]))
        forms.append(np.block([[real, imag], [-imag, real]]))
    exact = np.stack(forms)
    high = exact.astype(ml_dtypes.bfloat16)
    low = (exact - high.astype(np.float64)).astype(ml_dtypes.bfloat16)
    return np.stack([high, low], axis=1)


def split(x):
    high = x.astype(BF16)
    return high, (x - high.astype(F32)).astype(BF16)


def dot(a, b):
    return jnp.dot(a, b, preferred_element_type=F32)


def two_sided(tables, left, right, waves):
    size = waves[0][0].shape[0]
    x = jnp.concatenate(
        [jnp.concatenate([w[0] for w in waves], axis=1), jnp.concatenate([w[1] for w in waves], axis=1)], axis=0
    )
    high, low = split(x)
    t_high, t_low = tables[left, 0], tables[left, 1]
    t = dot(jnp.concatenate([t_high, t_high, t_low], axis=1), jnp.concatenate([high, low, high], axis=0))
    rows = []
    for j in range(len(waves)):
        cols = slice(j * size, (j + 1) * size)
        rows.append(jnp.concatenate([t[:size, cols], t[size:, cols]], axis=1))
    high, low = split(jnp.concatenate(rows, axis=0))
    t_high, t_low = tables[right, 0], tables[right, 1]
    y = dot(jnp.concatenate([high, low, high], axis=1), jnp.concatenate([t_high, t_high, t_low], axis=0))
    return [(y[j * size : (j + 1) * size, :size], y[j * size : (j + 1) * size, size:]) for j in range(len(waves))]


def times(a, b):
    return a[0] * b[0] - a[1] * b[1], a[0] * b[1] + a[1] * b[0]


def conj_times(a, b):
    return a[0] * b[0] + a[1] * b[1], a[0] * b[1] - a[1] * b[0]


def plus(a, b):
    return a[0] + b[0], a[1] + b[1]


class Many:
    def __init__(self, copies):
        self.copies = list(copies)

    def __getitem__(self, key):
        return Many(self.copies[key])

    def start(self):
        for copy in self.copies:
            copy.start()

    def wait_recv(self):
        for copy in self.copies:
            copy.wait_recv()

    def wait_send(self):
        for copy in self.copies:
            copy.wait_send()


class Bounded:
    def __init__(self, copy, sends, takes):
        self.copy, self.sends, self.takes = copy, sends, takes

    def start(self):
        pl.when(self.sends)(self.copy.start)

    def wait_recv(self):
        pl.when(self.takes)(self.copy.wait_recv)

    def wait_send(self):
        pl.when(self.sends)(self.copy.wait_send)


def kernel(
    ng,
    nm,
    tile,
    size,
    cap,
    offset_hbm,
    counts_hbm,
    object_ref,
    probe_hbm,
    measured_hbm,
    tables_hbm,
    grad_ref,
    probe_grad_ref,
    offset_ref,
    count_ref,
    counts_ref,
    probe_ref,
    measured_ref,
    tables,
    load_sem,
    ext_a,
    ext_b,
    rim_row,
    rim_col,
    land_row,
    land_col,
    land_corner,
    probe_rolled,
    first_cut,
    wave_mid,
    wave_back,
    pieces,
    probe_acc,
    land_pair,
    land_plane,
    part_sum,
    land_z,
    probe_sum,
    in_send,
    in_recv,
    own_sem,
    out_send,
    out_recv,
    pair_sem,
    plane_send,
    plane_recv,
    z_send,
    z_recv,
    back_send,
    back_recv,
):
    g, m = lax.axis_index("group"), lax.axis_index("member")
    left, right = (g, lax.rem(m + nm - 1, nm)), (g, lax.rem(m + 1, nm))
    up, down = (lax.rem(g + ng - 1, ng), m), (lax.rem(g + 1, ng), m)
    core, chip = lax.rem(m, 2), m // 2
    chips = nm // 2
    partner = (g, m + 1 - 2 * core)
    blocks = tile // size
    modes = probe_ref.shape[0] // 2
    ext = (ext_a, ext_b)

    def spot_of(start, length):
        return pl.ds(pl.multiple_of(start, 8), length)

    def remote(src, dst, send, recv, device):
        return pltpu.make_async_remote_copy(
            src_ref=src, dst_ref=dst, send_sem=send, recv_sem=recv, device_id=device, device_id_type=MESH
        )

    barrier = pltpu.get_barrier_semaphore()
    greeted = [up, down, left, right]
    greeted += [(g, 2 * lax.rem(chip + d, chips) + core) for d in range(1, chips)]
    greeted += [(lax.rem(g + d, ng), m) for d in range(2, ng - 1)]
    for device in greeted:
        pl.semaphore_signal(barrier, inc=1, device_id=device, device_id_type=MESH)
    pl.semaphore_wait(barrier, len(greeted))

    low, wide, edge = pl.ds(tile, size), pl.ds(0, tile), pl.ds(0, size)
    rest = pl.ds(size, tile - size)
    rims = []
    for s in range(2):
        rims.append(
            [
                remote(object_ref.at[s, :, edge, pl.ds(j * size, size)], ext[s].at[j, :, low], in_send.at[s, j], in_recv.at[s, j], up)
                for j in range(blocks)
            ]
            + [
                remote(object_ref.at[s, :, :, edge], ext[s].at[blocks, :, wide], in_send.at[s, blocks], in_recv.at[s, blocks], left),
                remote(ext[s].at[0, :, low], ext[s].at[blocks, :, low], in_send.at[s, blocks + 1], in_recv.at[s, blocks + 1], left),
            ]
        )
        for copy in rims[s][: blocks + 1]:
            copy.start()

    own_copies = [
        [
            pltpu.make_async_copy(object_ref.at[s, :, :, pl.ds(j * size, size)], ext[s].at[j, :, wide], own_sem.at[s, j])
            for j in range(blocks)
        ]
        for s in range(2)
    ]
    loads = [
        pltpu.make_async_copy(src, dst, load_sem.at[n])
        for n, (src, dst) in enumerate(
            (
                (offset_hbm, offset_ref),
                (probe_hbm, probe_ref),
                (tables_hbm, tables),
                (measured_hbm, measured_ref),
                (counts_hbm, count_ref),
                (counts_hbm, counts_ref),
            )
        )
    ]
    for copy in loads + own_copies[0] + own_copies[1]:
        copy.start()

    def place(p):
        row, col = offset_ref[0, 0, 0, p], offset_ref[0, 0, 1, p]
        return row, col // size, lax.rem(col, size)

    for copy in loads:
        copy.wait()

    def roll_probe(p, carry):
        _, _, cs = place(p)
        for plane in range(2 * modes):
            probe_rolled[p, plane] = pltpu.roll(probe_ref[plane], cs, axis=1)
        return carry

    lax.fori_loop(0, cap, roll_probe, 0)

    def from_start(cs):
        return lax.broadcasted_iota(jnp.int32, (size, size), 1) >= cs

    def cut(p, s):
        row, bj, cs = place(p)
        inside = from_start(cs)
        rows = pl.ds(row, size)
        return tuple(jnp.where(inside, ext[s][bj, plane, rows], ext[s][bj + 1, plane, rows]) for plane in range(2))

    def waves_of(ref, p):
        return [(ref[p, 2 * k], ref[p, 2 * k + 1]) for k in range(modes)]

    def store_waves(ref, p, waves):
        for k in range(modes):
            ref[p, 2 * k] = waves[k][0]
            ref[p, 2 * k + 1] = waves[k][1]

    def store_pieces(s, p, grad):
        _, _, cs = place(p)
        inside = from_start(cs)
        for plane in range(2):
            pieces[s, p, 0, plane, pl.ds(size, size)] = jnp.where(inside, grad[plane], 0.0)
            pieces[s, p, 1, plane, pl.ds(size, size)] = jnp.where(inside, 0.0, grad[plane])

    def clear_pieces(p, carry):
        for n in (0, 2):
            for s in range(2):
                pieces[s, p, :, :, pl.ds(n * size, size)] = jnp.zeros((2, 2, size, size), F32)
        return carry

    lax.fori_loop(0, cap, clear_pieces, 0)

    def assemble(s, i, j):
        total = None
        for p in range(cap):
            row, bj, _ = place(p)
            b = j - bj
            inside = (b >= 0) & (b <= 1)
            start = jnp.where(inside, jnp.clip((i + 1) * size - row, 0, 2 * size), 0)
            part = pieces[s, p, jnp.where(inside, b, 0), :, pl.ds(start, size)]
            total = part if total is None else total + part
        return total

    def span(t):
        return pl.ds(pl.multiple_of(t * size, size), size)

    def assemble_low(s, j):
        rim_row[s, :, :, span(j)] = assemble(s, blocks, j)

    def assemble_wide(s, i):
        rim_col[s, :, span(i)] = assemble(s, i, blocks)

    def assemble_own(s, t):
        i, j = t // blocks, lax.rem(t, blocks)
        grad_ref[s, :, span(i), span(j)] = assemble(s, i, j)

    def assemble_many(s, n, one):
        def step(t, carry):
            one(s, t)
            return carry

        lax.fori_loop(0, n, step, 0)

    fourier, fourier_conj, spread, spread_conj = (0, 1), (1, 0), (2, 3), (3, 2)

    def arrive(s):
        rims[s][0].wait_recv()
        rims[s][blocks + 1].start()
        for copy in own_copies[s]:
            copy.wait()
        for copy in rims[s][1:]:
            copy.wait_recv()

    arrive(0)

    def stage_one(t, carry):
        waves = []
        for q in range(PAIR):
            p = t * PAIR + q
            patch = cut(p, 0)
            first_cut[p, 0], first_cut[p, 1] = patch
            waves += [times(w, patch) for w in waves_of(probe_rolled, p)]
        waves = two_sided(tables, *spread, waves)
        for q in range(PAIR):
            store_waves(wave_mid, t * PAIR + q, waves[q * modes : (q + 1) * modes])
        return carry

    lax.fori_loop(0, cap // PAIR, stage_one, 0)

    arrive(1)

    own_count = count_ref[g, m]

    def stage_two(t, carry):
        patches, mids, waves = [], [], []
        for q in range(PAIR):
            p = t * PAIR + q
            patches.append(cut(p, 1))
            mids.append(waves_of(wave_mid, p))
            waves += [times(w, patches[q]) for w in mids[q]]
        far = two_sided(tables, *fourier, waves)
        waves = []
        for q in range(PAIR):
            p = t * PAIR + q
            intensity = None
            for w in far[q * modes : (q + 1) * modes]:
                power = w[0] * w[0] + w[1] * w[1]
                intensity = power if intensity is None else intensity + power
            valid = jnp.where(p < own_count, 2.0, 0.0).astype(F32)
            slope = valid * (1.0 - measured_ref[p] * lax.rsqrt(intensity + 1.0))
            waves += [(w[0] * slope, w[1] * slope) for w in far[q * modes : (q + 1) * modes]]
        back = two_sided(tables, *fourier_conj, waves)
        for q in range(PAIR):
            p = t * PAIR + q
            own = back[q * modes : (q + 1) * modes]
            grad = None
            for mid, w in zip(mids[q], own):
                term = conj_times(mid, w)
                grad = term if grad is None else plus(grad, term)
            store_pieces(1, p, grad)
            store_waves(wave_back, p, [conj_times(patches[q], w) for w in own])
        return carry

    lax.fori_loop(0, cap // PAIR, stage_two, 0)

    homes = []
    takes_rows, takes_cols = g > 0, m > 0

    def home_down(*args):
        return Bounded(remote(*args, down), g < ng - 1, takes_rows)

    def home_right(*args):
        return Bounded(remote(*args, right), m < nm - 1, takes_cols)

    for s in range(2):
        homes.append(
            (
                Many(
                    home_down(rim_row.at[s, :, :, part], land_row.at[s, :, :, part], out_send.at[s, 4 + j], out_recv.at[s, 4 + j])
                    for j, part in ((j, pl.ds((j + 1) * size, size)) for j in range(blocks - 1))
                ),
                home_right(rim_row.at[s, :, :, low], land_corner.at[s], out_send.at[s, 1], out_recv.at[s, 1]),
                Many(
                    home_right(rim_col.at[s, n], land_col.at[s, n], out_send.at[s, 2 * n], out_recv.at[s, 2 * n])
                    for n in range(2)
                ),
                home_down(rim_row.at[s, :, :, edge], land_row.at[s, :, :, edge], out_send.at[s, 3], out_recv.at[s, 3]),
            )
        )

    def send_corner(s):
        homes[s][1].wait_recv()

        @pl.when(takes_cols)
        def _():
            rim_row[s, :, :, edge] += land_corner[s]

        homes[s][3].start()

    assemble_many(1, blocks - 1, lambda s, t: assemble_low(s, t + 1))
    homes[1][0].start()
    assemble_low(1, blocks)
    homes[1][1].start()
    assemble_many(1, blocks, assemble_wide)
    homes[1][2].copies[0].start()
    assemble_low(1, 0)

    probe_acc[...] = jnp.zeros(probe_acc.shape, F32)

    def stage_three(t, carry):
        waves = []
        for q in range(PAIR):
            waves += waves_of(wave_back, t * PAIR + q)
        waves = two_sided(tables, *spread_conj, waves)
        turned_back = [[] for _ in range(PAIR * modes)]
        for q in range(PAIR):
            p = t * PAIR + q
            patch = (first_cut[p, 0], first_cut[p, 1])
            grad = None
            for k, (probe, w) in enumerate(zip(waves_of(probe_rolled, p), waves[q * modes : (q + 1) * modes])):
                term = conj_times(probe, w)
                grad = term if grad is None else plus(grad, term)
                turned = turned_back[q * modes + k]
                for plane, x in enumerate(conj_times(patch, w)):
                    turned.append(x)
            store_pieces(0, p, grad)
        for k in range(modes):
            for plane in range(2):
                total = None
                for q in range(PAIR):
                    _, _, cs = place(t * PAIR + q)
                    x = pltpu.roll(turned_back[q * modes + k][plane], lax.rem(size - cs, size), axis=1)
                    total = x if total is None else total + x
                probe_acc[pl.ds((2 * k + plane) * size, size), :] += total
        return carry

    lax.fori_loop(0, cap // PAIR, stage_three, 0)

    def finish(s):
        homes[s][2].wait_recv()

        @pl.when(takes_cols)
        def _():
            grad_ref[s, :, wide, edge] += land_col[s]

        homes[s][0].wait_recv()

        @pl.when(takes_rows)
        def _():
            grad_ref[s, :, edge, rest] += land_row[s, :, :, rest]

        homes[s][3].wait_recv()

        @pl.when(takes_rows)
        def _():
            grad_ref[s, :, edge, edge] += land_row[s, :, :, edge]

    rows = probe_acc.shape[0]
    half = rows // 2
    pair = remote(probe_acc.at[spot_of((1 - core) * half, half)], land_pair, pair_sem.at[0], pair_sem.at[1], partner)
    pair.start()
    assemble_low(0, blocks)
    homes[0][1].start()
    assemble_many(0, blocks, assemble_low)
    send_corner(1)
    pair.wait_recv()
    land_pair[...] += probe_acc[spot_of(core * half, half)]

    sent = [pair]

    def added(land, n, copies):
        for copy in copies:
            copy.wait_recv()
        sent.extend(copies)
        total = land[0]
        for t in range(1, n):
            total = total + land[t]
        return total

    part = half // chips
    copies = []
    for d in range(1, chips):
        other = lax.rem(chip + d, chips)
        to = (g, 2 * other + core)
        copies.append(remote(land_pair.at[spot_of(other * part, part)], land_plane.at[chip], plane_send.at[d], plane_recv.at[d], to))
        copies[-1].start()
    land_plane[chip] = land_pair[spot_of(chip * part, part)]
    assemble_many(0, blocks, assemble_wide)
    part_sum[...] = added(land_plane, chips, copies)
    land_z[g] = part_sum[...]
    copies = []
    for d in range(1, ng):
        to = (lax.rem(g + d, ng), m)
        copies.append(remote(part_sum, land_z.at[g], z_send.at[d], z_recv.at[d], to))
        copies[-1].start()
    homes[0][0].start()
    homes[1][2].copies[1].start()
    homes[0][2].copies[0].start()
    send_corner(0)
    assemble_many(1, blocks * blocks, assemble_own)
    positions = jnp.sum(counts_ref[...].astype(F32), keepdims=True)
    spot = spot_of(core * half + chip * part, part)
    probe_sum[spot] = added(land_z, ng, copies) / jnp.sqrt(positions)
    copies = []
    for d in range(1, chips):
        to = (g, 2 * lax.rem(chip + d, chips) + core)
        copies.append(remote(probe_sum.at[spot], probe_sum.at[spot], back_send.at[d], back_recv.at[d], to))
        copies[-1].start()

    homes[0][2].copies[1].start()
    assemble_many(0, blocks * blocks, assemble_own)
    finish(1)
    for copy in copies:
        copy.wait_recv()
    sent.extend(copies)
    mine = spot_of(core * half, half)
    share = remote(probe_sum.at[mine], probe_sum.at[mine], pair_sem.at[2], pair_sem.at[3], partner)
    share.start()
    finish(0)
    share.wait_recv()
    for plane in range(2 * modes):
        probe_grad_ref[plane] = probe_sum[pl.ds(plane * size, size), :]

    for s in range(2):
        for copy in [*rims[s], *homes[s]]:
            copy.wait_send()
    for copy in [*sent, share]:
        copy.wait_send()


def per_device(object_tiles, probe_modes, measured, slot_offset, slot_count):
    ng, nm = lax.axis_size("group"), lax.axis_size("member")
    tile = object_tiles.shape[-1]
    size = probe_modes.shape[-1]
    cap = measured.shape[2]
    planes = 2 * probe_modes.shape[0]
    ext = tile + size
    blocks = tile // size
    chips = nm // 2
    rows = planes * size
    step = rows // 2 // chips
    tables = jnp.asarray(make_tables(size))
    vmem = pl.BlockSpec(memory_space=pltpu.VMEM)
    hbm = pl.BlockSpec(memory_space=pltpu.HBM)
    dma = pltpu.SemaphoreType.DMA

    def body(*refs):
        kernel(ng, nm, tile, size, cap, *refs)

    grad, probe_grad = pl.pallas_call(
        body,
        out_shape=(
            pltpu.VMEM(object_tiles.shape, F32),
            pltpu.VMEM((planes, size, size), F32),
        ),
        in_specs=[hbm] * 6,
        out_specs=(vmem, vmem),
        scratch_shapes=[
            pltpu.SMEM((1, 1, 2, cap), jnp.int32),
            pltpu.SMEM(slot_count.shape, jnp.int32),
            pltpu.VMEM(slot_count.shape, jnp.int32),
            pltpu.VMEM((planes, size, size), F32),
            pltpu.VMEM((cap, size, size), F32),
            pltpu.VMEM(tables.shape, BF16),
            dma((6,)),
            pltpu.VMEM((blocks + 1, 2, ext, size), F32),
            pltpu.VMEM((blocks + 1, 2, ext, size), F32),
            pltpu.VMEM((2, 2, size, ext), F32),
            pltpu.VMEM((2, 2, tile, size), F32),
            pltpu.VMEM((2, 2, size, tile), F32),
            pltpu.VMEM((2, 2, tile, size), F32),
            pltpu.VMEM((2, 2, size, size), F32),
            pltpu.VMEM((cap, planes, size, size), F32),
            pltpu.VMEM((cap, 2, size, size), F32),
            pltpu.VMEM((cap, planes, size, size), F32),
            pltpu.VMEM((cap, planes, size, size), F32),
            pltpu.VMEM((2, cap, 2, 2, 3 * size, size), F32),
            pltpu.VMEM((rows, size), F32),
            pltpu.VMEM((rows // 2, size), F32),
            pltpu.VMEM((chips, step, size), F32),
            pltpu.VMEM((step, size), F32),
            pltpu.VMEM((ng, step, size), F32),
            pltpu.VMEM((rows, size), F32),
            dma((2, blocks + 2)),
            dma((2, blocks + 2)),
            dma((2, blocks)),
            dma((2, 3 + blocks)),
            dma((2, 3 + blocks)),
            dma((4,)),
            dma((chips,)),
            dma((chips,)),
            dma((ng,)),
            dma((ng,)),
            dma((chips,)),
            dma((chips,)),
        ],
        compiler_params=pltpu.CompilerParams(
            collective_id=0, has_side_effects=True, vmem_limit_bytes=48 * 1024 * 1024
        ),
    )(
        *(
            pltpu.with_memory_space_constraint(x, pltpu.HBM)
            for x in (
                jnp.swapaxes(slot_offset, 2, 3),
                slot_count,
                object_tiles,
                probe_modes.reshape(planes, size, size),
                measured.reshape(cap, size, size),
                tables,
            )
        ),
    )
    return grad, probe_grad.reshape(probe_modes.shape)


def solution(mesh):
    placed = (
        P(None, None, "group", "member"),
        P(),
        P("group", "member", None, None, None),
        P("group", "member", None, None),
        P(),
    )
    return jax.shard_map(
        per_device,
        mesh=mesh,
        in_specs=placed,
        out_specs=(P(None, None, "group", "member"), P()),
        check_vma=False,
    )
```
